32 devices in a mesh: groups: 2 (over x), dp: 16 (over z, y, core).
Axes of the slice: x: 2, y: 2, z: 4, core: 2. Of those that a mesh axis runs over, the one named last changes fastest.
Arguments:
- tiles: bfloat16 [160, 257, 1280], P(('groups', 'dp')), parts along dimension 0, may hold values from -6 to 6
- counts: int32 [32], P(('groups', 'dp')), parts along dimension 0, may hold values from 1 to 5, as said below
- w_query: bfloat16 [1280, 1280], P(None, 'dp'), may hold values from -10 to 10
- w_keyval: bfloat16 [1280, 2560], replicated, may hold values from -10 to 10
- w_out: bfloat16 [1280, 1280], P('dp'), may hold values from -0.15625 to 0.15625
- w_up: bfloat16 [1280, 5120], P(None, 'dp'), may hold values from -0.15625 to 0.15625
- w_down: bfloat16 [5120, 1280], P('dp'), may hold values from -0.078125 to 0.078125
- gain_attn: float32 [1280], replicated, may hold values from 0.1 to 1.9
- gain_mlp: float32 [1280], replicated, may hold values from 0.1 to 1.9
- gain_post: float32 [1280], replicated, may hold values from 0.1 to 1.9
- bias_post: float32 [1280], replicated, may hold values from -3 to 3
Outputs:
- pooled: float32 [32, 1280], P(('groups', 'dp')), parts along dimension 0
The draws below stay inside these ranges and needn't reach their ends.
There are 2 independent parts, one for each index of `groups`. The reference program is written for one: setup_inputs(seed, part) draws one part's arguments, and reference() takes and returns one part's arrays. A program takes and returns all parts, laid end to end along the dimension named above; an argument that names none is the same for every part. Nothing has to cross between parts.
Inputs may be any that keep to these rules, and one draw needn't show every extreme that they name: `counts`: some rollout has exactly 5 tiles and some exactly 1.
All inputs are finite; a program needn't handle non-finite values.
Results may differ from the reference program's by a relative error of at most 0.0046.
Values may be sent and summed in bfloat16 or wider, within the bound.
A program may use at most 64 MiB of HBM per device.

```python
import math
import jax
import jax.numpy as jnp
from jax import lax

D = 1280
HEADS = 16
HEAD_DIM = 80
FF = 5120
TOK = 257
MAXT = 5
ROLLOUTS = 16
TILE_SLOTS = 80


def draw_tiles(key, part):
    key = jax.random.fold_in(key, 11)
    first_key = jax.random.fold_in(key, 0)
    shape = (TILE_SLOTS, TOK, D)
    values = jax.random.normal(first_key, shape, jnp.float32)
    return jnp.clip(values, -6.0, 6.0).astype(jnp.bfloat16)


def draw_counts(key, part):
    key = jax.random.fold_in(key, 23)
    first_key, second_key, third_key = jax.random.split(key, 3)
    extra = jax.random.randint(first_key, (ROLLOUTS,), 0, MAXT) * jax.random.randint(second_key, (ROLLOUTS,), 0, 2)
    result = 1 + extra
    chosen = jax.random.randint(third_key, (), 0, ROLLOUTS)
    result = result.at[chosen].set(MAXT)
    result = result.at[(chosen + 1) % ROLLOUTS].set(1)
    return result.astype(jnp.int32)


def draw_w_query(key, part):
    key = jax.random.fold_in(key, 37)
    first_key = jax.random.fold_in(key, 0)
    noise = jnp.clip(jax.random.normal(first_key, (D, D), jnp.float32), -6.0, 6.0) / math.sqrt(D)
    values = noise
    return jnp.clip(values, -10.0, 10.0).astype(jnp.bfloat16)


def draw_w_keyval(key, part):
    key = jax.random.fold_in(key, 41)
    noise = jnp.clip(jax.random.normal(key, (D, 2 * D), jnp.float32), -6.0, 6.0) / math.sqrt(D)
    values = noise
    return jnp.clip(values, -10.0, 10.0).astype(jnp.bfloat16)


def block_levels(stream_key, dims, cuts, least, largest):
    def one(axis_at, blocks):
        draws = jax.random.uniform(jax.random.fold_in(jax.random.fold_in(stream_key, 6), axis_at), (blocks,), jnp.float32, least / len(cuts), largest / len(cuts))
        return jnp.repeat(jnp.exp(draws), dims[axis_at] // blocks).reshape((-1,) + (1,) * (len(dims) - axis_at - 1))

    loudness = one(*cuts[0])
    for cut in cuts[1:]:
        loudness = loudness * one(*cut)
    return loudness


def normal_values(stream_key, shape, deviation, bound, cuts=(), kind=jnp.bfloat16):
    entries = deviation * jax.random.normal(stream_key, shape, jnp.float32)
    if cuts:
        entries = entries * block_levels(stream_key, shape, cuts, -0.22, 0.18)
    return jnp.clip(entries, -bound, bound).astype(kind)


def setup_inputs(seed: int = 0, part: int = 0) -> dict:
    key_list = jax.random.split(jax.random.key(seed), 12)
    own_keys = jax.random.split(jax.random.fold_in(key_list[11], part), 12)
    tiles = draw_tiles(jax.random.fold_in(jax.random.fold_in(key_list[11], part), 71), part)
    counts = draw_counts(jax.random.fold_in(jax.random.fold_in(key_list[11], part), 71), part)
    w_query = draw_w_query(jax.random.fold_in(key_list[11], 71), part)
    w_keyval = draw_w_keyval(jax.random.fold_in(key_list[11], 71), part)
    w_out = normal_values(key_list[4], (D, D), D ** -0.5, 0.15625, ((0, 16),))
    w_up = normal_values(key_list[5], (D, FF), D ** -0.5, 0.15625, ((1, 16),))
    w_down = normal_values(key_list[6], (FF, D), FF ** -0.5, 0.078125, ((0, 16),))
    gain_attn = jnp.clip(1.0 + 0.18 * jax.random.normal(key_list[7], (D,), jnp.float32), 0.1, 1.9)
    gain_mlp = jnp.clip(1.0 + 0.18 * jax.random.normal(key_list[8], (D,), jnp.float32), 0.1, 1.9)
    gain_post = jnp.clip(1.0 + 0.18 * jax.random.normal(key_list[9], (D,), jnp.float32), 0.1, 1.9)
    bias_post = normal_values(key_list[10], (D,), 0.5, 3.0, (), jnp.float32)
    return dict(tiles=tiles, counts=counts, w_query=w_query, w_keyval=w_keyval, w_out=w_out, w_up=w_up, w_down=w_down, gain_attn=gain_attn, gain_mlp=gain_mlp, gain_post=gain_post, bias_post=bias_post)


epsilon = 1e-05

def layer_norm(values, gain):
    centre = lax.optimization_barrier(jnp.mean(values, axis=-1, keepdims=True))
    centred = values - centre
    spread_sq = lax.optimization_barrier(jnp.mean(centred * centred, axis=-1, keepdims=True))
    return centred * lax.rsqrt(spread_sq + epsilon) * gain.astype(jnp.float32)

def head_mix(query_row, keyval):
    keys = keyval[:, :D].astype(jnp.float32).reshape(-1, HEADS, HEAD_DIM)
    values = keyval[:, D:].astype(jnp.float32).reshape(-1, HEADS, HEAD_DIM)
    heads = query_row.astype(jnp.float32).reshape(HEADS, HEAD_DIM)
    scores = jnp.einsum('hd,thd->ht', heads, keys) / math.sqrt(HEAD_DIM)
    weights = jax.nn.softmax(scores, axis=-1).astype(jnp.bfloat16)
    mixing = jnp.einsum('ht,thd->hd', weights.astype(jnp.float32), values)
    return mixing.reshape(-1).astype(jnp.bfloat16)

def reference(tiles, counts, w_query, w_keyval, w_out, w_up, w_down, gain_attn, gain_mlp, gain_post, bias_post):

    def attend_tile(single):
        normed = layer_norm(single.astype(jnp.float32), gain_attn).astype(jnp.bfloat16)
        query_row = jnp.dot(normed[0:1], w_query, preferred_element_type=jnp.float32).astype(jnp.bfloat16)
        keyval = jnp.dot(normed, w_keyval, preferred_element_type=jnp.float32).astype(jnp.bfloat16)
        return head_mix(query_row[0], keyval)
    mixed = lax.map(attend_tile, tiles)
    settled = tiles[:, 0, :].astype(jnp.float32) + jnp.dot(mixed, w_out, preferred_element_type=jnp.float32)
    inner = layer_norm(settled, gain_mlp).astype(jnp.bfloat16)
    hidden = jax.nn.gelu(jnp.dot(inner, w_up, preferred_element_type=jnp.float32), approximate=False).astype(jnp.bfloat16)
    outcome = settled + jnp.dot(hidden, w_down, preferred_element_type=jnp.float32)
    final = layer_norm(outcome, gain_post) + bias_post.astype(jnp.float32)
    final = final.reshape(ROLLOUTS, MAXT, D)
    present = (jnp.arange(MAXT, dtype=jnp.int32)[None, :] < counts[:, None]).astype(jnp.float32)
    summed = lax.optimization_barrier(jnp.sum(final * present[:, :, None], axis=1))
    return summed / counts.astype(jnp.float32)[:, None]
```

```python
import functools
import math

import jax
import jax.numpy as jnp
from jax import lax
from jax.experimental import pallas as pl
from jax.experimental.pallas import tpu as pltpu
from jax.sharding import PartitionSpec as P

HEADS = 16
HEAD_DIM = 80
SLOTS = 5
ROWS = 16
WIDE = 512
GROUP = 256

epsilon = 1e-05
F32 = jnp.float32
BF16 = jnp.bfloat16
MESH = pl.DeviceIdType.MESH


def layer_norm(values, gain):
    centre = jnp.mean(values, axis=-1, keepdims=True)
    centred = values - centre
    spread_sq = jnp.mean(centred * centred, axis=-1, keepdims=True)
    return centred * lax.rsqrt(spread_sq + epsilon) * gain


def erf(x):
    x = jnp.clip(x, -3.832506856900711, 3.832506856900711)
    sq = x * x
    top = jnp.full_like(x, 0.00022905065861350646)
    for c in (
        0.0034082910107109506,
        0.050955695062380861,
        0.18520832239976145,
        1.128379143519084,
    ):
        top = top * sq + c
    low = jnp.full_like(x, -1.1791602954361697e-7)
    for c in (
        0.000023547966471313185,
        0.0010179625278914885,
        0.014070470171167667,
        0.11098505178285362,
        0.49746925110067538,
        1.0,
    ):
        low = low * sq + c
    return x * top / low


def gelu(x):
    return 0.5 * x * (1.0 + erf(x * math.sqrt(0.5)))


def dot(a, b):
    return jnp.dot(a, b, preferred_element_type=F32)


def dot_t(a, b):
    return lax.dot_general(a, b, (((1,), (1,)), ((), ())), preferred_element_type=F32)


def pack_rows(x):
    d = x.shape[1]
    last = jnp.concatenate([x[:, 2 * WIDE :], jnp.zeros((SLOTS, 3 * WIDE - d), F32)], axis=1)
    return jnp.concatenate(
        [x[:, :WIDE], x[:, WIDE : 2 * WIDE], last, jnp.zeros((1, WIDE), F32)], axis=0
    )


def unpack_rows(p, d):
    return jnp.concatenate(
        [p[0:SLOTS], p[SLOTS : 2 * SLOTS], p[2 * SLOTS : 3 * SLOTS, : d - 2 * WIDE]], axis=1
    )


def spread(packed, d):
    size = packed.shape[0]
    r = lax.broadcasted_iota(jnp.int32, (size, size), 0)
    c = lax.broadcasted_iota(jnp.int32, (size, size), 1)
    same = (r >> 4) == (c >> 4)
    rm = r & 15
    slot = rm - jnp.where(rm >= 5, 5, 0) - jnp.where(rm >= 10, 5, 0) - jnp.where(rm >= 15, 5, 0)
    cm = c & 15
    out = []
    for k in range(3):
        pick = jnp.where(same & (cm == slot + 5 * k), 1.0, 0.0).astype(BF16)
        src = packed if k < 2 else packed[:, : d - 2 * WIDE]
        out.append(dot(pick, src).astype(BF16))
    return jnp.concatenate(out, axis=1)


def fold(y):
    size, d = y.shape
    rm = lax.broadcasted_iota(jnp.int32, (size, WIDE), 0) & 15
    last = jnp.concatenate([y[:, 2 * WIDE :], jnp.zeros((size, 3 * WIDE - d), F32)], axis=1)
    return jnp.where(rm < 5, y[:, :WIDE], jnp.where(rm < 10, y[:, WIDE : 2 * WIDE], last))


def kernel(
    n,
    tiles, counts, w_query, w_keyval, w_out, w_up, w_down, gain_attn, gain_mlp, gain_post, bias_post,
    out,
    first_v, tiles_v, normed_v, wq_v, wk_v, wv_v, wo_v, wu_v, wd_v,
    rows_r, q_s, q_r, mix_s, mix_r, out_s, out_r, inner_r, feed_s, feed_r,
    load_sem, send_sem, recv_sem,
):
    me = lax.axis_index("dp")
    tok, d = tiles.shape[1], tiles.shape[2]
    cw = w_query.shape[1]
    total = n * ROWS
    groups = max(total // GROUP, 1)
    size = total // groups

    loads = []

    def load(src, dst):
        copy = pltpu.make_async_copy(src, dst, load_sem.at[len(loads)])
        copy.start()
        loads.append(copy)
        return copy

    load_first = load(tiles.at[:, pl.ds(0, 16), :], first_v)
    load_q = load(w_query, wq_v)
    load_tiles = [load(tiles.at[s], tiles_v.at[s]) for s in range(SLOTS)]
    load_k = load(w_keyval.at[:, pl.ds(0, d)], wk_v)
    load_v = load(w_keyval.at[:, pl.ds(d, d)], wv_v)
    load_o = load(w_out, wo_v)
    load_u = load(w_up, wu_v)
    load_d = load(w_down, wd_v)

    barrier = pltpu.get_barrier_semaphore()

    def greet(k, _):
        peer = lax.rem(me + k, n)
        pl.semaphore_signal(barrier, inc=1, device_id={"dp": peer}, device_id_type=MESH)
        return 0

    lax.fori_loop(1, n, greet, 0)

    def send_all(src_at, dst, phase):
        def body(k, _):
            peer = lax.rem(me + k, n)
            pltpu.make_async_remote_copy(
                src_ref=src_at(peer),
                dst_ref=dst.at[me],
                send_sem=send_sem.at[phase],
                recv_sem=recv_sem.at[phase],
                device_id={"dp": peer},
                device_id_type=MESH,
            ).start()
            return 0

        lax.fori_loop(1, n, body, 0)

    def wait_all(ref, sem):
        part = ref.at[pl.ds(0, n - 1)]
        pltpu.make_async_copy(part, part, sem).wait()

    g_attn = gain_attn[...].reshape(1, d)

    load_first.wait()
    first = jnp.concatenate([first_v[s, 0:1, :].astype(F32) for s in range(SLOTS)], axis=0)
    rows_r[me] = pack_rows(layer_norm(first, g_attn)).astype(BF16)
    pl.semaphore_wait(barrier, n - 1)
    send_all(lambda peer: rows_r.at[me], rows_r, 0)

    def norm_tile(s):
        load_tiles[s].wait()

        def body(i, _):
            at = pl.ds(pl.multiple_of(i * 32, 32), 32)
            normed_v[s, at, :] = layer_norm(tiles_v[s, at, :].astype(F32), g_attn).astype(BF16)
            return 0

        lax.fori_loop(0, tok // 32, body, 0, unroll=2)
        whole = tok // 32 * 32
        rest = tok - whole
        tail = layer_norm(tiles_v[s, whole:tok, :].astype(F32), g_attn)
        tail = jnp.concatenate(
            [tail, jnp.zeros((normed_v.shape[1] - tok, d), F32)], axis=0
        )
        normed_v[s, whole:, :] = tail.astype(BF16)

    for s in range(3):
        norm_tile(s)

    load_q.wait()
    wait_all(rows_r, recv_sem.at[0])
    for g in range(groups):
        owners = size // ROWS
        packed = rows_r[g * owners : (g + 1) * owners].reshape(size, WIDE)
        q = dot(spread(packed, d), wq_v[...]).astype(BF16)
        q_s[g * owners : (g + 1) * owners] = q.reshape(owners, ROWS, cw)
    send_all(lambda peer: q_s.at[peer], q_r, 1)
    q_r[me] = q_s[me]

    for s in range(3, SLOTS):
        norm_tile(s)

    load_k.wait()
    wait_all(q_r, recv_sem.at[1])
    query = jnp.concatenate([q_r[i].astype(F32) for i in range(n)], axis=1)
    head_row = lax.broadcasted_iota(jnp.int32, (HEADS, d), 0)
    lane = lax.broadcasted_iota(jnp.int32, (HEADS, d), 1)
    own_head = (lane >= head_row * HEAD_DIM) & (lane < (head_row + 1) * HEAD_DIM)
    apart = jnp.concatenate(
        [jnp.where(own_head, query[s : s + 1], 0.0).astype(BF16) for s in range(SLOTS)], axis=0
    )
    keyed = dot_t(apart, wk_v[...]).astype(BF16)
    padded = normed_v.shape[1]
    real = lax.broadcasted_iota(jnp.int32, (HEADS, padded), 1) < tok
    context = []
    for s in range(SLOTS):
        scores = dot_t(keyed[s * HEADS : (s + 1) * HEADS], normed_v[s]) / math.sqrt(HEAD_DIM)
        scores = jnp.where(real, scores, -jnp.inf)
        weights = jnp.exp(scores - jnp.max(scores, axis=-1, keepdims=True))
        weights = weights / jnp.sum(weights, axis=-1, keepdims=True)
        context.append(dot(weights.astype(BF16), normed_v[s]).astype(BF16))
    load_v.wait()
    valued = dot(jnp.concatenate(context, axis=0), wv_v[...])
    mixed = jnp.concatenate(
        [
            jnp.sum(
                jnp.where(own_head, valued[s * HEADS : (s + 1) * HEADS], 0.0),
                axis=0,
                keepdims=True,
            )
            for s in range(SLOTS)
        ],
        axis=0,
    )
    thrice = jnp.concatenate([mixed, mixed, mixed, mixed[0:1]], axis=0)
    for i in range(n):
        mix_s[i] = thrice[:, i * cw : (i + 1) * cw].astype(BF16)
    send_all(lambda peer: mix_s.at[peer], mix_r, 2)
    mix_r[me] = mix_s[me]

    load_o.wait()
    wait_all(mix_r, recv_sem.at[2])
    owners = size // ROWS
    for g in range(groups):
        at = slice(g * owners, (g + 1) * owners)
        part = dot(mix_r[at].reshape(size, cw), wo_v[...])
        out_s[at] = fold(part).astype(BF16).reshape(owners, ROWS, WIDE)
    send_all(lambda peer: out_s.at[peer], out_r, 3)
    out_r[me] = out_s[me]
    wait_all(out_r, recv_sem.at[3])

    def total_of(ref):
        acc = ref[0].astype(F32)
        for i in range(1, n):
            acc = acc + ref[i].astype(F32)
        return unpack_rows(acc, d)

    settled = first + total_of(out_r)
    inner = layer_norm(settled, gain_mlp[...].reshape(1, d))
    inner_r[me] = pack_rows(inner).astype(BF16)
    send_all(lambda peer: inner_r.at[me], inner_r, 4)
    load_u.wait()
    load_d.wait()
    wait_all(inner_r, recv_sem.at[4])
    for g in range(groups):
        at = slice(g * owners, (g + 1) * owners)
        rows = spread(inner_r[at].reshape(size, WIDE), d)
        hidden = gelu(dot(rows, wu_v[...])).astype(BF16)
        feed_s[at] = fold(dot(hidden, wd_v[...])).astype(BF16).reshape(owners, ROWS, WIDE)
    send_all(lambda peer: feed_s.at[peer], feed_r, 5)
    feed_r[me] = feed_s[me]
    wait_all(feed_r, recv_sem.at[5])

    outcome = settled + total_of(feed_r)
    final = layer_norm(outcome, gain_post[...].reshape(1, d)) + bias_post[...].reshape(1, d)
    count = counts[0]
    present = lax.broadcasted_iota(jnp.int32, (SLOTS, d), 0) < count
    summed = jnp.sum(jnp.where(present, final, 0.0), axis=0, keepdims=True)
    out[...] = summed / jnp.full((1, d), count, jnp.int32).astype(F32)

    for phase, ref in enumerate((rows_r, q_s, mix_s, out_s, inner_r, feed_s)):
        wait_all(ref, send_sem.at[phase])


def shards(
    tiles, counts, w_query, w_keyval, w_out, w_up, w_down, gain_attn, gain_mlp, gain_post, bias_post
):
    n = lax.axis_size("dp")
    slots, tok, d = tiles.shape
    cw = w_query.shape[1]
    padded = (tok + 15) // 16 * 16
    anywhere = pl.BlockSpec(memory_space=pl.ANY)
    vmem = pl.BlockSpec(memory_space=pltpu.VMEM)
    smem = pl.BlockSpec(memory_space=pltpu.SMEM)
    message = pltpu.VMEM((n, ROWS, WIDE), BF16)
    narrow = pltpu.VMEM((n, ROWS, cw), BF16)
    return pl.pallas_call(
        functools.partial(kernel, n),
        out_shape=jax.ShapeDtypeStruct((counts.shape[0], d), F32),
        in_specs=[anywhere, smem] + [anywhere] * 5 + [vmem] * 4,
        out_specs=vmem,
        scratch_shapes=[
            pltpu.VMEM((slots, 16, d), BF16),
            pltpu.VMEM((slots, tok, d), BF16),
            pltpu.VMEM((slots, padded, d), BF16),
            pltpu.VMEM(w_query.shape, BF16),
            pltpu.VMEM((d, d), BF16),
            pltpu.VMEM((d, d), BF16),
            pltpu.VMEM(w_out.shape, BF16),
            pltpu.VMEM(w_up.shape, BF16),
            pltpu.VMEM(w_down.shape, BF16),
            message, narrow, narrow, narrow, narrow, message, message, message, message, message,
            pltpu.SemaphoreType.DMA((12,)),
            pltpu.SemaphoreType.DMA((6,)),
            pltpu.SemaphoreType.DMA((6,)),
        ],
        compiler_params=pltpu.CompilerParams(
            collective_id=0, has_side_effects=True, vmem_limit_bytes=50 * 1024 * 1024
        ),
    )(tiles, counts, w_query, w_keyval, w_out, w_up, w_down, gain_attn, gain_mlp, gain_post, bias_post)


def solution(mesh):
    placed = (
        P(("groups", "dp"), None, None),
        P(("groups", "dp")),
        P(None, "dp"),
        P(),
        P("dp", None),
        P(None, "dp"),
        P("dp", None),
        P(),
        P(),
        P(),
        P(),
    )
    return jax.shard_map(
        shards, mesh=mesh, in_specs=placed, out_specs=P(("groups", "dp"), None), check_vma=False
    )
```

```python
import functools
import math

import jax
import jax.numpy as jnp
from jax import lax
from jax.experimental import pallas as pl
from jax.experimental.pallas import tpu as pltpu
from jax.sharding import PartitionSpec as P

HEADS = 16
HEAD_DIM = 80
SLOTS = 5
ROWS = 16
WIDE = 512
GROUP = 256

epsilon = 1e-05
F32 = jnp.float32
BF16 = jnp.bfloat16
MESH = pl.DeviceIdType.MESH


def layer_norm(values, gain):
    centre = jnp.mean(values, axis=-1, keepdims=True)
    centred = values - centre
    spread_sq = jnp.mean(centred * centred, axis=-1, keepdims=True)
    return centred * lax.rsqrt(spread_sq + epsilon) * gain


def erf(x):
    x = jnp.clip(x, -3.832506856900711, 3.832506856900711)
    sq = x * x
    top = jnp.full_like(x, 0.00022905065861350646)
    for c in (
        0.0034082910107109506,
        0.050955695062380861,
        0.18520832239976145,
        1.128379143519084,
    ):
        top = top * sq + c
    low = jnp.full_like(x, -1.1791602954361697e-7)
    for c in (
        0.000023547966471313185,
        0.0010179625278914885,
        0.014070470171167667,
        0.11098505178285362,
        0.49746925110067538,
        1.0,
    ):
        low = low * sq + c
    return x * top / low


def gelu(x):
    return 0.5 * x * (1.0 + erf(x * math.sqrt(0.5)))


def dot(a, b):
    return jnp.dot(a, b, preferred_element_type=F32)


def dot_t(a, b):
    return lax.dot_general(a, b, (((1,), (1,)), ((), ())), preferred_element_type=F32)


def pack_rows(x):
    d = x.shape[1]
    last = jnp.concatenate([x[:, 2 * WIDE :], jnp.zeros((SLOTS, 3 * WIDE - d), F32)], axis=1)
    return jnp.concatenate(
        [x[:, :WIDE], x[:, WIDE : 2 * WIDE], last, jnp.zeros((1, WIDE), F32)], axis=0
    )


def unpack_rows(p, d):
    return jnp.concatenate(
        [p[0:SLOTS], p[SLOTS : 2 * SLOTS], p[2 * SLOTS : 3 * SLOTS, : d - 2 * WIDE]], axis=1
    )


def spread(packed, d):
    size = packed.shape[0]
    r = lax.broadcasted_iota(jnp.int32, (size, size), 0)
    c = lax.broadcasted_iota(jnp.int32, (size, size), 1)
    same = (r >> 4) == (c >> 4)
    rm = r & 15
    slot = rm - jnp.where(rm >= 5, 5, 0) - jnp.where(rm >= 10, 5, 0) - jnp.where(rm >= 15, 5, 0)
    cm = c & 15
    out = []
    for k in range(3):
        pick = jnp.where(same & (cm == slot + 5 * k), 1.0, 0.0).astype(BF16)
        src = packed if k < 2 else packed[:, : d - 2 * WIDE]
        out.append(dot(pick, src).astype(BF16))
    return jnp.concatenate(out, axis=1)


def fold(y):
    size, d = y.shape
    rm = lax.broadcasted_iota(jnp.int32, (size, WIDE), 0) & 15
    last = jnp.concatenate([y[:, 2 * WIDE :], jnp.zeros((size, 3 * WIDE - d), F32)], axis=1)
    return jnp.where(rm < 5, y[:, :WIDE], jnp.where(rm < 10, y[:, WIDE : 2 * WIDE], last))


def kernel(
    n,
    tiles, counts, w_query, w_keyval, w_out, w_up, w_down, gain_attn, gain_mlp, gain_post, bias_post,
    out,
    gains_v, first_v, tiles_v, normed_v, wq_v, wk_v, wv_v, wo_v, wu_v, wd_v,
    rows_r, q_s, q_r, mix_s, mix_r, out_s, out_r, inner_r, feed_s, feed_r,
    load_sem, send_sem, recv_sem,
):
    me = lax.axis_index("dp")
    tok, d = tiles.shape[1], tiles.shape[2]
    cw = w_query.shape[0]
    total = n * ROWS
    groups = max(total // GROUP, 1)
    size = total // groups

    loads = []

    def load(src, dst):
        copy = pltpu.make_async_copy(src, dst, load_sem.at[len(loads)])
        copy.start()
        loads.append(copy)
        return copy

    load_gains = [
        load(ref, gains_v.at[i])
        for i, ref in enumerate((gain_attn, gain_mlp, gain_post, bias_post))
    ]
    load_first = load(tiles.at[:, pl.ds(0, 16), :], first_v)
    load_q = load(w_query, wq_v)
    load_tiles = [load(tiles.at[s], tiles_v.at[s]) for s in range(SLOTS)]
    load_k = load(w_keyval.at[:, pl.ds(0, d)], wk_v)
    load_v = load(w_keyval.at[:, pl.ds(d, d)], wv_v)
    load_o = load(w_out, wo_v)
    load_u = load(w_up, wu_v)
    load_d = load(w_down, wd_v)

    barrier = pltpu.get_barrier_semaphore()

    def greet(k, _):
        peer = lax.rem(me + k, n)
        pl.semaphore_signal(barrier, inc=1, device_id={"dp": peer}, device_id_type=MESH)
        return 0

    lax.fori_loop(1, n, greet, 0)

    def send_all(src_at, dst, phase):
        def body(k, _):
            peer = lax.rem(me + k, n)
            pltpu.make_async_remote_copy(
                src_ref=src_at(peer),
                dst_ref=dst.at[me],
                send_sem=send_sem.at[phase],
                recv_sem=recv_sem.at[phase],
                device_id={"dp": peer},
                device_id_type=MESH,
            ).start()
            return 0

        lax.fori_loop(1, n, body, 0)

    def wait_all(ref, sem):
        part = ref.at[pl.ds(0, n - 1)]
        pltpu.make_async_copy(part, part, sem).wait()

    for copy in load_gains:
        copy.wait()
    g_attn, g_mlp, g_post, b_post = [gains_v[i].reshape(1, d) for i in range(4)]

    load_first.wait()
    first = jnp.concatenate([first_v[s, 0:1, :].astype(F32) for s in range(SLOTS)], axis=0)
    rows_r[me] = pack_rows(layer_norm(first, g_attn)).astype(BF16)
    pl.semaphore_wait(barrier, n - 1)
    send_all(lambda peer: rows_r.at[me], rows_r, 0)

    def norm_tile(s):
        load_tiles[s].wait()

        def body(i, _):
            at = pl.ds(pl.multiple_of(i * 32, 32), 32)
            normed_v[s, at, :] = layer_norm(tiles_v[s, at, :].astype(F32), g_attn).astype(BF16)
            return 0

        lax.fori_loop(0, tok // 32, body, 0, unroll=2)
        whole = tok // 32 * 32
        rest = tok - whole
        tail = layer_norm(tiles_v[s, whole:tok, :].astype(F32), g_attn)
        tail = jnp.concatenate(
            [tail, jnp.zeros((normed_v.shape[1] - tok, d), F32)], axis=0
        )
        normed_v[s, whole:, :] = tail.astype(BF16)

    for s in range(3):
        norm_tile(s)

    load_q.wait()
    wait_all(rows_r, recv_sem.at[0])
    for g in range(groups):
        owners = size // ROWS
        packed = rows_r[g * owners : (g + 1) * owners].reshape(size, WIDE)
        q = dot_t(spread(packed, d), wq_v[...]).astype(BF16)
        q_s[g * owners : (g + 1) * owners] = q.reshape(owners, ROWS, cw)
    send_all(lambda peer: q_s.at[peer], q_r, 1)
    q_r[me] = q_s[me]

    for s in range(3, SLOTS):
        norm_tile(s)

    load_k.wait()
    wait_all(q_r, recv_sem.at[1])
    query = jnp.concatenate([q_r[i].astype(F32) for i in range(n)], axis=1)
    head_row = lax.broadcasted_iota(jnp.int32, (HEADS, d), 0)
    lane = lax.broadcasted_iota(jnp.int32, (HEADS, d), 1)
    own_head = (lane >= head_row * HEAD_DIM) & (lane < (head_row + 1) * HEAD_DIM)
    apart = jnp.concatenate(
        [jnp.where(own_head, query[s : s + 1], 0.0).astype(BF16) for s in range(SLOTS)], axis=0
    )
    keyed = dot_t(apart, wk_v[...]).astype(BF16)
    padded = normed_v.shape[1]
    real = lax.broadcasted_iota(jnp.int32, (HEADS, padded), 1) < tok
    context = []
    for s in range(SLOTS):
        scores = dot_t(keyed[s * HEADS : (s + 1) * HEADS], normed_v[s]) / math.sqrt(HEAD_DIM)
        scores = jnp.where(real, scores, -jnp.inf)
        weights = jnp.exp(scores - jnp.max(scores, axis=-1, keepdims=True))
        weights = weights / jnp.sum(weights, axis=-1, keepdims=True)
        context.append(dot(weights.astype(BF16), normed_v[s]).astype(BF16))
    load_v.wait()
    valued = dot(jnp.concatenate(context, axis=0), wv_v[...])
    mixed = jnp.concatenate(
        [
            jnp.sum(
                jnp.where(own_head, valued[s * HEADS : (s + 1) * HEADS], 0.0),
                axis=0,
                keepdims=True,
            )
            for s in range(SLOTS)
        ],
        axis=0,
    )
    thrice = jnp.concatenate([mixed, mixed, mixed, mixed[0:1]], axis=0)
    for i in range(n):
        mix_s[i] = thrice[:, i * cw : (i + 1) * cw].astype(BF16)
    send_all(lambda peer: mix_s.at[peer], mix_r, 2)
    mix_r[me] = mix_s[me]

    load_o.wait()
    wait_all(mix_r, recv_sem.at[2])
    owners = size // ROWS
    for g in range(groups):
        at = slice(g * owners, (g + 1) * owners)
        part = dot(mix_r[at].reshape(size, cw), wo_v[...])
        out_s[at] = fold(part).astype(BF16).reshape(owners, ROWS, WIDE)
    send_all(lambda peer: out_s.at[peer], out_r, 3)
    out_r[me] = out_s[me]
    wait_all(out_r, recv_sem.at[3])

    def total_of(ref):
        acc = ref[0].astype(F32)
        for i in range(1, n):
            acc = acc + ref[i].astype(F32)
        return unpack_rows(acc, d)

    settled = first + total_of(out_r)
    inner = layer_norm(settled, g_mlp)
    inner_r[me] = pack_rows(inner).astype(BF16)
    send_all(lambda peer: inner_r.at[me], inner_r, 4)
    load_u.wait()
    load_d.wait()
    wait_all(inner_r, recv_sem.at[4])
    for g in range(groups):
        at = slice(g * owners, (g + 1) * owners)
        rows = spread(inner_r[at].reshape(size, WIDE), d)
        hidden = gelu(dot_t(rows, wu_v[...])).astype(BF16)
        feed_s[at] = fold(dot(hidden, wd_v[...])).astype(BF16).reshape(owners, ROWS, WIDE)
    send_all(lambda peer: feed_s.at[peer], feed_r, 5)
    feed_r[me] = feed_s[me]
    wait_all(feed_r, recv_sem.at[5])

    outcome = settled + total_of(feed_r)
    final = layer_norm(outcome, g_post) + b_post
    count = counts[0]
    present = lax.broadcasted_iota(jnp.int32, (SLOTS, d), 0) < count
    summed = jnp.sum(jnp.where(present, final, 0.0), axis=0, keepdims=True)
    out[...] = summed / jnp.full((1, d), count, jnp.int32).astype(F32)

    for phase, ref in enumerate((rows_r, q_s, mix_s, out_s, inner_r, feed_s)):
        wait_all(ref, send_sem.at[phase])


def shards(
    tiles, counts, w_query, w_keyval, w_out, w_up, w_down, gain_attn, gain_mlp, gain_post, bias_post
):
    n = lax.axis_size("dp")
    slots, tok, d = tiles.shape
    cw = w_query.shape[1]
    w_query, w_up = w_query.T, w_up.T
    padded = (tok + 15) // 16 * 16
    anywhere = pl.BlockSpec(memory_space=pl.ANY)
    vmem = pl.BlockSpec(memory_space=pltpu.VMEM)
    smem = pl.BlockSpec(memory_space=pltpu.SMEM)
    message = pltpu.VMEM((n, ROWS, WIDE), BF16)
    narrow = pltpu.VMEM((n, ROWS, cw), BF16)
    return pl.pallas_call(
        functools.partial(kernel, n),
        out_shape=jax.ShapeDtypeStruct((counts.shape[0], d), F32),
        in_specs=[anywhere, smem] + [anywhere] * 9,
        out_specs=vmem,
        scratch_shapes=[
            pltpu.VMEM((4, d), F32),
            pltpu.VMEM((slots, 16, d), BF16),
            pltpu.VMEM((slots, tok, d), BF16),
            pltpu.VMEM((slots, padded, d), BF16),
            pltpu.VMEM(w_query.shape, BF16),
            pltpu.VMEM((d, d), BF16),
            pltpu.VMEM((d, d), BF16),
            pltpu.VMEM(w_out.shape, BF16),
            pltpu.VMEM(w_up.shape, BF16),
            pltpu.VMEM(w_down.shape, BF16),
            message, narrow, narrow, narrow, narrow, message, message, message, message, message,
            pltpu.SemaphoreType.DMA((16,)),
            pltpu.SemaphoreType.DMA((6,)),
            pltpu.SemaphoreType.DMA((6,)),
        ],
        compiler_params=pltpu.CompilerParams(
            collective_id=0, has_side_effects=True, vmem_limit_bytes=60 * 1024 * 1024
        ),
    )(tiles, counts, w_query, w_keyval, w_out, w_up, w_down, gain_attn, gain_mlp, gain_post, bias_post)


def solution(mesh):
    placed = (
        P(("groups", "dp"), None, None),
        P(("groups", "dp")),
        P(None, "dp"),
        P(),
        P("dp", None),
        P(None, "dp"),
        P("dp", None),
        P(),
        P(),
        P(),
        P(),
    )
    return jax.shard_map(
        shards, mesh=mesh, in_specs=placed, out_specs=P(("groups", "dp"), None), check_vma=False
    )
```

```python
import functools
import math

import jax
import jax.numpy as jnp
from jax import lax
from jax.experimental import pallas as pl
from jax.experimental.pallas import tpu as pltpu
from jax.sharding import PartitionSpec as P

HEADS = 16
HEAD_DIM = 80
SLOTS = 5
ROWS = 16
WIDE = 512
GROUP = 256

epsilon = 1e-05
F32 = jnp.float32
BF16 = jnp.bfloat16
MESH = pl.DeviceIdType.MESH


def layer_norm(values, gain):
    centre = jnp.mean(values, axis=-1, keepdims=True)
    centred = values - centre
    spread_sq = jnp.mean(centred * centred, axis=-1, keepdims=True)
    return centred * lax.rsqrt(spread_sq + epsilon) * gain


def erf(x):
    x = jnp.clip(x, -3.832506856900711, 3.832506856900711)
    sq = x * x
    top = jnp.full_like(x, 0.00022905065861350646)
    for c in (
        0.0034082910107109506,
        0.050955695062380861,
        0.18520832239976145,
        1.128379143519084,
    ):
        top = top * sq + c
    low = jnp.full_like(x, -1.1791602954361697e-7)
    for c in (
        0.000023547966471313185,
        0.0010179625278914885,
        0.014070470171167667,
        0.11098505178285362,
        0.49746925110067538,
        1.0,
    ):
        low = low * sq + c
    return x * top / low


def gelu(x):
    return 0.5 * x * (1.0 + erf(x * math.sqrt(0.5)))


def dot(a, b):
    return jnp.dot(a, b, preferred_element_type=F32)


def dot_t(a, b):
    return lax.dot_general(a, b, (((1,), (1,)), ((), ())), preferred_element_type=F32)


def pack_rows(x):
    d = x.shape[1]
    last = jnp.concatenate([x[:, 2 * WIDE :], jnp.zeros((SLOTS, 3 * WIDE - d), F32)], axis=1)
    return jnp.concatenate(
        [x[:, :WIDE], x[:, WIDE : 2 * WIDE], last, jnp.zeros((1, WIDE), F32)], axis=0
    )


def unpack_rows(p, d):
    return jnp.concatenate(
        [p[0:SLOTS], p[SLOTS : 2 * SLOTS], p[2 * SLOTS : 3 * SLOTS, : d - 2 * WIDE]], axis=1
    )


def spread(packed, d):
    size = packed.shape[0]
    r = lax.broadcasted_iota(jnp.int32, (size, size), 0)
    c = lax.broadcasted_iota(jnp.int32, (size, size), 1)
    same = (r >> 4) == (c >> 4)
    rm = r & 15
    slot = rm - jnp.where(rm >= 5, 5, 0) - jnp.where(rm >= 10, 5, 0) - jnp.where(rm >= 15, 5, 0)
    cm = c & 15
    out = []
    for k in range(3):
        pick = jnp.where(same & (cm == slot + 5 * k), 1.0, 0.0).astype(BF16)
        src = packed if k < 2 else packed[:, : d - 2 * WIDE]
        out.append(dot(pick, src).astype(BF16))
    return jnp.concatenate(out, axis=1)


def fold(y):
    size, d = y.shape
    rm = lax.broadcasted_iota(jnp.int32, (size, WIDE), 0) & 15
    last = jnp.concatenate([y[:, 2 * WIDE :], jnp.zeros((size, 3 * WIDE - d), F32)], axis=1)
    return jnp.where(rm < 5, y[:, :WIDE], jnp.where(rm < 10, y[:, WIDE : 2 * WIDE], last))


def kernel(
    n,
    tiles, counts, w_query, w_keyval, w_out, w_up, w_down, gain_attn, gain_mlp, gain_post, bias_post,
    out,
    gains_v, first_v, tiles_v, normed_v, wq_v, wk_v, wv_v, wo_v, wu_v, wd_v,
    rows_r, q_s, q_r, mix_s, mix_r, out_s, out_r, inner_r, feed_s, feed_r,
    load_sem, send_sem, recv_sem, weight_send, weight_recv,
):
    me = lax.axis_index("dp")
    tok, d = tiles.shape[1], tiles.shape[2]
    cw = w_query.shape[0]
    core = lax.rem(me, 2)
    sibling = me + 1 - 2 * core
    chips = n // 2
    chip = lax.div(me, 2)
    total = chips * ROWS
    groups = max(total // GROUP, 1)
    size = total // groups

    loads = []

    def load(src, dst):
        copy = pltpu.make_async_copy(src, dst, load_sem.at[len(loads)])
        copy.start()
        loads.append(copy)
        return copy

    load_gains = [
        load(ref, gains_v.at[i])
        for i, ref in enumerate((gain_attn, gain_mlp, gain_post, bias_post))
    ]
    load_first = load(tiles.at[:, pl.ds(0, 16), :], first_v)
    load_q = load(w_query, wq_v.at[core])
    load_tiles = [load(tiles.at[s], tiles_v.at[s]) for s in range(SLOTS)]
    load_k = load(w_keyval.at[:, pl.ds(0, d)], wk_v)
    load_v = load(w_keyval.at[:, pl.ds(d, d)], wv_v)
    load_o = load(w_out, wo_v.at[core])
    load_u = load(w_up, wu_v.at[core])
    load_d = load(w_down, wd_v.at[core])

    barrier = pltpu.get_barrier_semaphore()

    def greet(k, _):
        peer = lax.rem(chip + k, chips) * 2 + core
        pl.semaphore_signal(barrier, inc=1, device_id={"dp": peer}, device_id_type=MESH)
        return 0

    pl.semaphore_signal(barrier, inc=1, device_id={"dp": sibling}, device_id_type=MESH)
    lax.fori_loop(1, chips, greet, 0)

    def send_all(src_at, dst, phase):
        def body(k, _):
            peer = lax.rem(chip + k, chips)
            pltpu.make_async_remote_copy(
                src_ref=src_at(peer),
                dst_ref=dst.at[chip],
                send_sem=send_sem.at[phase],
                recv_sem=recv_sem.at[phase],
                device_id={"dp": peer * 2 + core},
                device_id_type=MESH,
            ).start()
            return 0

        lax.fori_loop(1, chips, body, 0)

    def wait_all(ref, sem):
        part = ref.at[pl.ds(0, chips - 1)]
        pltpu.make_async_copy(part, part, sem).wait()

    for copy in load_gains:
        copy.wait()
    g_attn, g_mlp, g_post, b_post = [gains_v[i].reshape(1, d) for i in range(4)]

    load_first.wait()
    first = jnp.concatenate([first_v[s, 0:1, :].astype(F32) for s in range(SLOTS)], axis=0)
    rows_r[chip] = pack_rows(layer_norm(first, g_attn)).astype(BF16)
    pl.semaphore_wait(barrier, chips)
    send_all(lambda peer: rows_r.at[chip], rows_r, 0)

    shared = []
    for k, (src, dst) in enumerate(((w_query, wq_v), (w_out, wo_v), (w_up, wu_v), (w_down, wd_v))):
        copy = pltpu.make_async_remote_copy(
            src_ref=src,
            dst_ref=dst.at[core],
            send_sem=weight_send.at[k],
            recv_sem=weight_recv.at[k],
            device_id={"dp": sibling},
            device_id_type=MESH,
        )
        copy.start()
        shared.append(copy)
    share_q, share_o, share_u, share_d = shared

    def norm_tile(s):
        load_tiles[s].wait()

        def body(i, _):
            at = pl.ds(pl.multiple_of(i * 32, 32), 32)
            normed_v[s, at, :] = layer_norm(tiles_v[s, at, :].astype(F32), g_attn).astype(BF16)
            return 0

        lax.fori_loop(0, tok // 32, body, 0, unroll=2)
        whole = tok // 32 * 32
        rest = tok - whole
        tail = layer_norm(tiles_v[s, whole:tok, :].astype(F32), g_attn)
        tail = jnp.concatenate(
            [tail, jnp.zeros((normed_v.shape[1] - tok, d), F32)], axis=0
        )
        normed_v[s, whole:, :] = tail.astype(BF16)

    for s in range(3):
        norm_tile(s)

    load_q.wait()
    share_q.wait_recv()
    wait_all(rows_r, recv_sem.at[0])
    for g in range(groups):
        owners = size // ROWS
        packed = rows_r[g * owners : (g + 1) * owners].reshape(size, WIDE)
        whole = spread(packed, d)
        for h in range(2):
            q = dot_t(whole, wq_v[h]).astype(BF16)
            q_s[g * owners : (g + 1) * owners, h] = q.reshape(owners, ROWS, cw)
    send_all(lambda peer: q_s.at[peer], q_r, 1)
    q_r[chip] = q_s[chip]

    for s in range(3, SLOTS):
        norm_tile(s)

    load_k.wait()
    wait_all(q_r, recv_sem.at[1])
    query = jnp.concatenate([q_r[i, h].astype(F32) for i in range(chips) for h in range(2)], axis=1)
    head_row = lax.broadcasted_iota(jnp.int32, (HEADS, d), 0)
    lane = lax.broadcasted_iota(jnp.int32, (HEADS, d), 1)
    own_head = (lane >= head_row * HEAD_DIM) & (lane < (head_row + 1) * HEAD_DIM)
    apart = jnp.concatenate(
        [jnp.where(own_head, query[s : s + 1], 0.0).astype(BF16) for s in range(SLOTS)], axis=0
    )
    keyed = dot_t(apart, wk_v[...]).astype(BF16)
    padded = normed_v.shape[1]
    real = lax.broadcasted_iota(jnp.int32, (HEADS, padded), 1) < tok
    context = []
    for s in range(SLOTS):
        scores = dot_t(keyed[s * HEADS : (s + 1) * HEADS], normed_v[s]) / math.sqrt(HEAD_DIM)
        scores = jnp.where(real, scores, -jnp.inf)
        weights = jnp.exp(scores - jnp.max(scores, axis=-1, keepdims=True))
        weights = weights / jnp.sum(weights, axis=-1, keepdims=True)
        context.append(dot(weights.astype(BF16), normed_v[s]).astype(BF16))
    load_v.wait()
    valued = dot(jnp.concatenate(context, axis=0), wv_v[...])
    mixed = jnp.concatenate(
        [
            jnp.sum(
                jnp.where(own_head, valued[s * HEADS : (s + 1) * HEADS], 0.0),
                axis=0,
                keepdims=True,
            )
            for s in range(SLOTS)
        ],
        axis=0,
    )
    thrice = jnp.concatenate([mixed, mixed, mixed, mixed[0:1]], axis=0)
    for i in range(n):
        mix_s[i // 2, i % 2] = thrice[:, i * cw : (i + 1) * cw].astype(BF16)
    send_all(lambda peer: mix_s.at[peer], mix_r, 2)
    mix_r[chip] = mix_s[chip]

    load_o.wait()
    share_o.wait_recv()
    wait_all(mix_r, recv_sem.at[2])
    owners = size // ROWS
    for g in range(groups):
        at = slice(g * owners, (g + 1) * owners)
        part = dot(mix_r[at, 0].reshape(size, cw), wo_v[0])
        part = part + dot(mix_r[at, 1].reshape(size, cw), wo_v[1])
        out_s[at] = fold(part).astype(BF16).reshape(owners, ROWS, WIDE)
    send_all(lambda peer: out_s.at[peer], out_r, 3)
    out_r[chip] = out_s[chip]
    wait_all(out_r, recv_sem.at[3])

    def total_of(ref):
        acc = ref[0].astype(F32)
        for i in range(1, chips):
            acc = acc + ref[i].astype(F32)
        return unpack_rows(acc, d)

    settled = first + total_of(out_r)
    inner = layer_norm(settled, g_mlp)
    inner_r[chip] = pack_rows(inner).astype(BF16)
    send_all(lambda peer: inner_r.at[chip], inner_r, 4)
    load_u.wait()
    share_u.wait_recv()
    load_d.wait()
    share_d.wait_recv()
    wait_all(inner_r, recv_sem.at[4])
    for g in range(groups):
        at = slice(g * owners, (g + 1) * owners)
        rows = spread(inner_r[at].reshape(size, WIDE), d)
        hidden = gelu(dot_t(rows, wu_v[...].reshape(-1, d))).astype(BF16)
        feed_s[at] = fold(dot(hidden, wd_v[...].reshape(-1, d))).astype(BF16).reshape(owners, ROWS, WIDE)
    send_all(lambda peer: feed_s.at[peer], feed_r, 5)
    feed_r[chip] = feed_s[chip]
    wait_all(feed_r, recv_sem.at[5])

    outcome = settled + total_of(feed_r)
    final = layer_norm(outcome, g_post) + b_post
    count = counts[0]
    present = lax.broadcasted_iota(jnp.int32, (SLOTS, d), 0) < count
    summed = jnp.sum(jnp.where(present, final, 0.0), axis=0, keepdims=True)
    out[...] = summed / jnp.full((1, d), count, jnp.int32).astype(F32)

    for phase, ref in enumerate((rows_r, q_s, mix_s, out_s, inner_r, feed_s)):
        wait_all(ref, send_sem.at[phase])
    for copy in shared:
        copy.wait_send()


def shards(
    tiles, counts, w_query, w_keyval, w_out, w_up, w_down, gain_attn, gain_mlp, gain_post, bias_post
):
    n = lax.axis_size("dp")
    slots, tok, d = tiles.shape
    cw = w_query.shape[1]
    w_query, w_up = w_query.T, w_up.T
    padded = (tok + 15) // 16 * 16
    anywhere = pl.BlockSpec(memory_space=pl.ANY)
    vmem = pl.BlockSpec(memory_space=pltpu.VMEM)
    smem = pl.BlockSpec(memory_space=pltpu.SMEM)
    message = pltpu.VMEM((n // 2, ROWS, WIDE), BF16)
    narrow = pltpu.VMEM((n // 2, 2, ROWS, cw), BF16)
    return pl.pallas_call(
        functools.partial(kernel, n),
        out_shape=jax.ShapeDtypeStruct((counts.shape[0], d), F32),
        in_specs=[anywhere, smem] + [anywhere] * 9,
        out_specs=vmem,
        scratch_shapes=[
            pltpu.VMEM((4, d), F32),
            pltpu.VMEM((slots, 16, d), BF16),
            pltpu.VMEM((slots, tok, d), BF16),
            pltpu.VMEM((slots, padded, d), BF16),
            pltpu.VMEM((2,) + w_query.shape, BF16),
            pltpu.VMEM((d, d), BF16),
            pltpu.VMEM((d, d), BF16),
            pltpu.VMEM((2,) + w_out.shape, BF16),
            pltpu.VMEM((2,) + w_up.shape, BF16),
            pltpu.VMEM((2,) + w_down.shape, BF16),
            message, narrow, narrow, narrow, narrow, message, message, message, message, message,
            pltpu.SemaphoreType.DMA((16,)),
            pltpu.SemaphoreType.DMA((6,)),
            pltpu.SemaphoreType.DMA((6,)),
            pltpu.SemaphoreType.DMA((4,)),
            pltpu.SemaphoreType.DMA((4,)),
        ],
        compiler_params=pltpu.CompilerParams(
            collective_id=0, has_side_effects=True, vmem_limit_bytes=60 * 1024 * 1024
        ),
    )(tiles, counts, w_query, w_keyval, w_out, w_up, w_down, gain_attn, gain_mlp, gain_post, bias_post)


def solution(mesh):
    placed = (
        P(("groups", "dp"), None, None),
        P(("groups", "dp")),
        P(None, "dp"),
        P(),
        P("dp", None),
        P(None, "dp"),
        P("dp", None),
        P(),
        P(),
        P(),
        P(),
    )
    return jax.shard_map(
        shards, mesh=mesh, in_specs=placed, out_specs=P(("groups", "dp"), None), check_vma=False
    )
```

```python
import functools
import math

import jax
import jax.numpy as jnp
from jax import lax
from jax.experimental import pallas as pl
from jax.experimental.pallas import tpu as pltpu
from jax.sharding import PartitionSpec as P

HEADS = 16
HEAD_DIM = 80
SLOTS = 5
ROWS = 16
WIDE = 512
GROUP = 256

epsilon = 1e-05
F32 = jnp.float32
BF16 = jnp.bfloat16
MESH = pl.DeviceIdType.MESH


def layer_norm(values, gain):
    centre = jnp.mean(values, axis=-1, keepdims=True)
    centred = values - centre
    spread_sq = jnp.mean(centred * centred, axis=-1, keepdims=True)
    return centred * lax.rsqrt(spread_sq + epsilon) * gain


def erf(x):
    x = jnp.clip(x, -3.832506856900711, 3.832506856900711)
    sq = x * x
    top = jnp.full_like(x, 0.00022905065861350646)
    for c in (
        0.0034082910107109506,
        0.050955695062380861,
        0.18520832239976145,
        1.128379143519084,
    ):
        top = top * sq + c
    low = jnp.full_like(x, -1.1791602954361697e-7)
    for c in (
        0.000023547966471313185,
        0.0010179625278914885,
        0.014070470171167667,
        0.11098505178285362,
        0.49746925110067538,
        1.0,
    ):
        low = low * sq + c
    return x * top / low


def gelu(x):
    return 0.5 * x * (1.0 + erf(x * math.sqrt(0.5)))


def dot(a, b):
    return jnp.dot(a, b, preferred_element_type=F32)


def dot_t(a, b):
    return lax.dot_general(a, b, (((1,), (1,)), ((), ())), preferred_element_type=F32)


def pack_rows(x):
    d = x.shape[1]
    last = jnp.concatenate([x[:, 2 * WIDE :], jnp.zeros((SLOTS, 3 * WIDE - d), F32)], axis=1)
    return jnp.concatenate(
        [x[:, :WIDE], x[:, WIDE : 2 * WIDE], last, jnp.zeros((1, WIDE), F32)], axis=0
    )


def unpack_rows(p, d):
    return jnp.concatenate(
        [p[0:SLOTS], p[SLOTS : 2 * SLOTS], p[2 * SLOTS : 3 * SLOTS, : d - 2 * WIDE]], axis=1
    )


def spread(packed, d):
    size = packed.shape[0]
    r = lax.broadcasted_iota(jnp.int32, (size, size), 0)
    c = lax.broadcasted_iota(jnp.int32, (size, size), 1)
    same = (r >> 4) == (c >> 4)
    rm = r & 15
    slot = rm - jnp.where(rm >= 5, 5, 0) - jnp.where(rm >= 10, 5, 0) - jnp.where(rm >= 15, 5, 0)
    cm = c & 15
    out = []
    for k in range(3):
        pick = jnp.where(same & (cm == slot + 5 * k), 1.0, 0.0).astype(BF16)
        src = packed if k < 2 else packed[:, : d - 2 * WIDE]
        out.append(dot(pick, src).astype(BF16))
    return jnp.concatenate(out, axis=1)


def fold(y):
    size, d = y.shape
    rm = lax.broadcasted_iota(jnp.int32, (size, WIDE), 0) & 15
    last = jnp.concatenate([y[:, 2 * WIDE :], jnp.zeros((size, 3 * WIDE - d), F32)], axis=1)
    return jnp.where(rm < 5, y[:, :WIDE], jnp.where(rm < 10, y[:, WIDE : 2 * WIDE], last))


def kernel(
    n,
    tiles, counts, w_query, w_keyval, w_out, w_up, w_down, gain_attn, gain_mlp, gain_post, bias_post,
    out,
    gains_v, first_v, tiles_v, normed_v, wq_v, wk_v, wv_v, wo_v, wu_v, wd_v,
    rows_r, q_s, q_r, mix_s, mix_r, out_s, out_r, inner_r, feed_s, feed_r,
    load_sem, send_sem, recv_sem, weight_send, weight_recv,
):
    me = lax.axis_index("dp")
    tok, d = tiles.shape[1], tiles.shape[2]
    cw = w_query.shape[0]
    core = lax.rem(me, 2)
    sibling = me + 1 - 2 * core
    chips = n // 2
    chip = lax.div(me, 2)
    total = chips * ROWS
    groups = max(total // GROUP, 1)
    size = total // groups

    loads = []

    def load(src, dst):
        copy = pltpu.make_async_copy(src, dst, load_sem.at[len(loads)])
        copy.start()
        loads.append(copy)
        return copy

    load_gains = [
        load(ref, gains_v.at[i])
        for i, ref in enumerate((gain_attn, gain_mlp, gain_post, bias_post))
    ]
    load_first = load(tiles.at[:, pl.ds(0, 16), :], first_v)
    load_q = load(w_query, wq_v.at[core])
    load_tiles = [load(tiles.at[s], tiles_v.at[s]) for s in range(SLOTS)]
    load_k = load(w_keyval.at[:, pl.ds(0, d)], wk_v)
    load_v = load(w_keyval.at[:, pl.ds(d, d)], wv_v)
    load_o = load(w_out, wo_v.at[core])
    load_u = load(w_up, wu_v.at[core])
    load_d = load(w_down, wd_v.at[core])

    barrier = pltpu.get_barrier_semaphore()

    def greet(k, _):
        peer = lax.rem(chip + k, chips) * 2 + core
        pl.semaphore_signal(barrier, inc=1, device_id={"dp": peer}, device_id_type=MESH)
        return 0

    pl.semaphore_signal(barrier, inc=1, device_id={"dp": sibling}, device_id_type=MESH)
    lax.fori_loop(1, chips, greet, 0)

    def send_all(src_at, dst, phase):
        def body(k, _):
            away = 1 + lax.rem(k + chips // 2 - 2, chips - 1)
            peer = lax.rem(chip + away, chips)
            pltpu.make_async_remote_copy(
                src_ref=src_at(peer),
                dst_ref=dst.at[chip],
                send_sem=send_sem.at[phase],
                recv_sem=recv_sem.at[phase],
                device_id={"dp": peer * 2 + core},
                device_id_type=MESH,
            ).start()
            return 0

        lax.fori_loop(1, chips, body, 0)

    def wait_all(ref, sem):
        part = ref.at[pl.ds(0, chips - 1)]
        pltpu.make_async_copy(part, part, sem).wait()

    for copy in load_gains:
        copy.wait()
    g_attn, g_mlp, g_post, b_post = [gains_v[i].reshape(1, d) for i in range(4)]

    load_first.wait()
    first = jnp.concatenate([first_v[s, 0:1, :].astype(F32) for s in range(SLOTS)], axis=0)
    rows_r[chip] = pack_rows(layer_norm(first, g_attn)).astype(BF16)
    pl.semaphore_wait(barrier, chips)
    send_all(lambda peer: rows_r.at[chip], rows_r, 0)

    shared = []
    for k, (src, dst) in enumerate(((w_query, wq_v), (w_out, wo_v), (w_up, wu_v), (w_down, wd_v))):
        copy = pltpu.make_async_remote_copy(
            src_ref=src,
            dst_ref=dst.at[core],
            send_sem=weight_send.at[k],
            recv_sem=weight_recv.at[k],
            device_id={"dp": sibling},
            device_id_type=MESH,
        )
        copy.start()
        shared.append(copy)
    share_q, share_o, share_u, share_d = shared

    whole = tok // 256 * 256

    def norm_tile(s):
        load_tiles[s].wait()

        def body(i, _):
            at = pl.ds(pl.multiple_of(i * 32, 32), 32)
            normed_v[s, at, :] = layer_norm(tiles_v[s, at, :].astype(F32), g_attn).astype(BF16)
            return 0

        lax.fori_loop(0, whole // 32, body, 0, unroll=2)
        tail = layer_norm(tiles_v[s, whole:tok, :].astype(F32), g_attn)
        tail = jnp.concatenate(
            [tail, jnp.zeros((normed_v.shape[1] - tok, d), F32)], axis=0
        )
        normed_v[s, whole:, :] = tail.astype(BF16)

    for s in range(3):
        norm_tile(s)

    load_q.wait()
    share_q.wait_recv()
    wait_all(rows_r, recv_sem.at[0])
    for g in range(groups):
        owners = size // ROWS
        packed = rows_r[g * owners : (g + 1) * owners].reshape(size, WIDE)
        each = spread(packed, d)
        for h in range(2):
            q = dot_t(each, wq_v[h]).astype(BF16)
            q_s[g * owners : (g + 1) * owners, h] = q.reshape(owners, ROWS, cw)
    send_all(lambda peer: q_s.at[peer], q_r, 1)
    q_r[chip] = q_s[chip]

    for s in range(3, SLOTS):
        norm_tile(s)

    load_k.wait()
    wait_all(q_r, recv_sem.at[1])
    query = jnp.concatenate([q_r[i, h].astype(F32) for i in range(chips) for h in range(2)], axis=1)
    head_row = lax.broadcasted_iota(jnp.int32, (HEADS, d), 0)
    lane = lax.broadcasted_iota(jnp.int32, (HEADS, d), 1)
    own_head = (lane >= head_row * HEAD_DIM) & (lane < (head_row + 1) * HEAD_DIM)
    apart = jnp.concatenate(
        [jnp.where(own_head, query[s : s + 1], 0.0).astype(BF16) for s in range(SLOTS)], axis=0
    )
    keyed = dot_t(apart, wk_v[...]).astype(BF16)
    parts = [keyed[s * HEADS : (s + 1) * HEADS] for s in range(SLOTS)]
    scores = jnp.concatenate([dot_t(parts[s], normed_v[s, :whole, :]) for s in range(SLOTS)], axis=0)
    wide_keyed = keyed.astype(F32)
    extra = []
    for t in range(whole, tok):
        rows = [
            jnp.broadcast_to(normed_v[s, t : t + 1, :].astype(F32), (HEADS, d)) for s in range(SLOTS)
        ]
        extra.append(
            (rows, jnp.sum(wide_keyed * jnp.concatenate(rows, axis=0), axis=-1, keepdims=True))
        )
    scale = 1.0 / math.sqrt(HEAD_DIM)
    scores = scores * scale
    peak = jnp.max(scores, axis=-1, keepdims=True)
    for _, score in extra:
        peak = jnp.maximum(peak, score * scale)
    weights = jnp.exp(scores - peak)
    last = [jnp.exp(score * scale - peak) for _, score in extra]
    norm = 1.0 / (jnp.sum(weights, axis=-1, keepdims=True) + sum(last))
    weights = (weights * norm).astype(BF16)
    last = [(w * norm).astype(BF16).astype(F32) for w in last]
    context = []
    for s in range(SLOTS):
        at = slice(s * HEADS, (s + 1) * HEADS)
        mean = dot(weights[at], normed_v[s, :whole, :])
        for (rows, _), w in zip(extra, last):
            mean = mean + w[at] * rows[s]
        context.append(mean.astype(BF16))
    load_v.wait()
    valued = dot(jnp.concatenate(context, axis=0), wv_v[...])
    mixed = jnp.concatenate(
        [
            jnp.sum(
                jnp.where(own_head, valued[s * HEADS : (s + 1) * HEADS], 0.0),
                axis=0,
                keepdims=True,
            )
            for s in range(SLOTS)
        ],
        axis=0,
    )
    thrice = jnp.concatenate([mixed, mixed, mixed, mixed[0:1]], axis=0)
    for i in range(n):
        mix_s[i // 2, i % 2] = thrice[:, i * cw : (i + 1) * cw].astype(BF16)
    send_all(lambda peer: mix_s.at[peer], mix_r, 2)
    mix_r[chip] = mix_s[chip]

    load_o.wait()
    share_o.wait_recv()
    wait_all(mix_r, recv_sem.at[2])
    owners = size // ROWS
    for g in range(groups):
        at = slice(g * owners, (g + 1) * owners)
        part = dot(mix_r[at, 0].reshape(size, cw), wo_v[0])
        part = part + dot(mix_r[at, 1].reshape(size, cw), wo_v[1])
        out_s[at] = fold(part).astype(BF16).reshape(owners, ROWS, WIDE)
    send_all(lambda peer: out_s.at[peer], out_r, 3)
    out_r[chip] = out_s[chip]
    wait_all(out_r, recv_sem.at[3])

    def total_of(ref):
        acc = ref[0].astype(F32)
        for i in range(1, chips):
            acc = acc + ref[i].astype(F32)
        return unpack_rows(acc, d)

    settled = first + total_of(out_r)
    inner = layer_norm(settled, g_mlp)
    inner_r[chip] = pack_rows(inner).astype(BF16)
    send_all(lambda peer: inner_r.at[chip], inner_r, 4)
    load_u.wait()
    share_u.wait_recv()
    load_d.wait()
    share_d.wait_recv()
    wait_all(inner_r, recv_sem.at[4])
    for g in range(groups):
        at = slice(g * owners, (g + 1) * owners)
        rows = spread(inner_r[at].reshape(size, WIDE), d)
        hidden = gelu(dot_t(rows, wu_v[...].reshape(-1, d))).astype(BF16)
        feed_s[at] = fold(dot(hidden, wd_v[...].reshape(-1, d))).astype(BF16).reshape(owners, ROWS, WIDE)
    send_all(lambda peer: feed_s.at[peer], feed_r, 5)
    feed_r[chip] = feed_s[chip]
    wait_all(feed_r, recv_sem.at[5])

    outcome = settled + total_of(feed_r)
    final = layer_norm(outcome, g_post) + b_post
    count = counts[0]
    present = lax.broadcasted_iota(jnp.int32, (SLOTS, d), 0) < count
    summed = jnp.sum(jnp.where(present, final, 0.0), axis=0, keepdims=True)
    out[...] = summed / jnp.full((1, d), count, jnp.int32).astype(F32)

    for phase, ref in enumerate((rows_r, q_s, mix_s, out_s, inner_r, feed_s)):
        wait_all(ref, send_sem.at[phase])
    for copy in shared:
        copy.wait_send()


def shards(
    tiles, counts, w_query, w_keyval, w_out, w_up, w_down, gain_attn, gain_mlp, gain_post, bias_post
):
    n = lax.axis_size("dp")
    slots, tok, d = tiles.shape
    cw = w_query.shape[1]
    w_query, w_up = w_query.T, w_up.T
    padded = (tok + 15) // 16 * 16
    anywhere = pl.BlockSpec(memory_space=pl.ANY)
    vmem = pl.BlockSpec(memory_space=pltpu.VMEM)
    smem = pl.BlockSpec(memory_space=pltpu.SMEM)
    message = pltpu.VMEM((n // 2, ROWS, WIDE), BF16)
    narrow = pltpu.VMEM((n // 2, 2, ROWS, cw), BF16)
    return pl.pallas_call(
        functools.partial(kernel, n),
        out_shape=jax.ShapeDtypeStruct((counts.shape[0], d), F32),
        in_specs=[anywhere, smem] + [anywhere] * 9,
        out_specs=vmem,
        scratch_shapes=[
            pltpu.VMEM((4, d), F32),
            pltpu.VMEM((slots, 16, d), BF16),
            pltpu.VMEM((slots, tok, d), BF16),
            pltpu.VMEM((slots, padded, d), BF16),
            pltpu.VMEM((2,) + w_query.shape, BF16),
            pltpu.VMEM((d, d), BF16),
            pltpu.VMEM((d, d), BF16),
            pltpu.VMEM((2,) + w_out.shape, BF16),
            pltpu.VMEM((2,) + w_up.shape, BF16),
            pltpu.VMEM((2,) + w_down.shape, BF16),
            message, narrow, narrow, narrow, narrow, message, message, message, message, message,
            pltpu.SemaphoreType.DMA((16,)),
            pltpu.SemaphoreType.DMA((6,)),
            pltpu.SemaphoreType.DMA((6,)),
            pltpu.SemaphoreType.DMA((4,)),
            pltpu.SemaphoreType.DMA((4,)),
        ],
        compiler_params=pltpu.CompilerParams(
            collective_id=0, has_side_effects=True, vmem_limit_bytes=60 * 1024 * 1024
        ),
    )(tiles, counts, w_query, w_keyval, w_out, w_up, w_down, gain_attn, gain_mlp, gain_post, bias_post)


def solution(mesh):
    placed = (
        P(("groups", "dp"), None, None),
        P(("groups", "dp")),
        P(None, "dp"),
        P(),
        P("dp", None),
        P(None, "dp"),
        P("dp", None),
        P(),
        P(),
        P(),
        P(),
    )
    return jax.shard_map(
        shards, mesh=mesh, in_specs=placed, out_specs=P(("groups", "dp"), None), check_vma=False
    )
```

```python
import functools
import math

import jax
import jax.numpy as jnp
from jax import lax
from jax.experimental import pallas as pl
from jax.experimental.pallas import tpu as pltpu
from jax.sharding import PartitionSpec as P

HEADS = 16
HEAD_DIM = 80
SLOTS = 5
ROWS = 16
WIDE = 512
GROUP = 256

epsilon = 1e-05
F32 = jnp.float32
BF16 = jnp.bfloat16
MESH = pl.DeviceIdType.MESH


def layer_norm(values, gain):
    centre = jnp.mean(values, axis=-1, keepdims=True)
    centred = values - centre
    spread_sq = jnp.mean(centred * centred, axis=-1, keepdims=True)
    return centred * lax.rsqrt(spread_sq + epsilon) * gain


def erf(x):
    x = jnp.clip(x, -3.832506856900711, 3.832506856900711)
    sq = x * x
    top = jnp.full_like(x, 0.00022905065861350646)
    for c in (
        0.0034082910107109506,
        0.050955695062380861,
        0.18520832239976145,
        1.128379143519084,
    ):
        top = top * sq + c
    low = jnp.full_like(x, -1.1791602954361697e-7)
    for c in (
        0.000023547966471313185,
        0.0010179625278914885,
        0.014070470171167667,
        0.11098505178285362,
        0.49746925110067538,
        1.0,
    ):
        low = low * sq + c
    return x * top / low


def gelu(x):
    return 0.5 * x * (1.0 + erf(x * math.sqrt(0.5)))


def dot(a, b):
    return jnp.dot(a, b, preferred_element_type=F32)


def dot_t(a, b):
    return lax.dot_general(a, b, (((1,), (1,)), ((), ())), preferred_element_type=F32)


def pack_rows(x):
    d = x.shape[1]
    last = jnp.concatenate([x[:, 2 * WIDE :], jnp.zeros((SLOTS, 3 * WIDE - d), F32)], axis=1)
    return jnp.concatenate(
        [x[:, :WIDE], x[:, WIDE : 2 * WIDE], last, jnp.zeros((1, WIDE), F32)], axis=0
    )


def unpack_rows(p, d):
    return jnp.concatenate(
        [p[0:SLOTS], p[SLOTS : 2 * SLOTS], p[2 * SLOTS : 3 * SLOTS, : d - 2 * WIDE]], axis=1
    )


def spread(packed, d):
    size = packed.shape[0]
    r = lax.broadcasted_iota(jnp.int32, (size, size), 0)
    c = lax.broadcasted_iota(jnp.int32, (size, size), 1)
    same = (r >> 4) == (c >> 4)
    rm = r & 15
    slot = rm - jnp.where(rm >= 5, 5, 0) - jnp.where(rm >= 10, 5, 0) - jnp.where(rm >= 15, 5, 0)
    cm = c & 15
    out = []
    for k in range(3):
        pick = jnp.where(same & (cm == slot + 5 * k), 1.0, 0.0).astype(BF16)
        src = packed if k < 2 else packed[:, : d - 2 * WIDE]
        out.append(dot(pick, src).astype(BF16))
    return jnp.concatenate(out, axis=1)


def fold(y):
    size, d = y.shape
    rm = lax.broadcasted_iota(jnp.int32, (size, WIDE), 0) & 15
    last = jnp.concatenate([y[:, 2 * WIDE :], jnp.zeros((size, 3 * WIDE - d), F32)], axis=1)
    return jnp.where(rm < 5, y[:, :WIDE], jnp.where(rm < 10, y[:, WIDE : 2 * WIDE], last))


def kernel(
    n,
    tiles, counts, w_query, w_keyval, w_out, w_up, w_down, gain_attn, gain_mlp, gain_post, bias_post,
    out,
    gains_v, first_v, tiles_v, normed_v, wq_v, wk_v, wv_v, wo_v, wu_v, wd_v,
    rows_r, q_s, q_r, mix_s, mix_r, out_s, out_r, inner_r, feed_s, feed_r,
    load_sem, send_sem, recv_sem, weight_send, weight_recv,
):
    me = lax.axis_index("dp")
    tok, d = tiles.shape[1], tiles.shape[2]
    cw = w_query.shape[0]
    core = lax.rem(me, 2)
    sibling = me + 1 - 2 * core
    chips = n // 2
    chip = lax.div(me, 2)
    total = chips * ROWS
    groups = max(total // GROUP, 1)
    size = total // groups

    barrier = pltpu.get_barrier_semaphore()

    def greet(k, _):
        peer = lax.rem(chip + k, chips) * 2 + core
        pl.semaphore_signal(barrier, inc=1, device_id={"dp": peer}, device_id_type=MESH)
        return 0

    pl.semaphore_signal(barrier, inc=1, device_id={"dp": sibling}, device_id_type=MESH)
    lax.fori_loop(1, chips, greet, 0)

    loads = []

    def load(src, dst):
        copy = pltpu.make_async_copy(src, dst, load_sem.at[len(loads)])
        copy.start()
        loads.append(copy)
        return copy

    load_gains = [
        load(ref, gains_v.at[i])
        for i, ref in enumerate((gain_attn, gain_mlp, gain_post, bias_post))
    ]
    load_first = load(tiles.at[:, pl.ds(0, 16), :], first_v)
    load_q = load(w_query, wq_v.at[core])
    load_tiles = [load(tiles.at[s], tiles_v.at[s]) for s in range(SLOTS)]
    load_k = load(w_keyval.at[:, pl.ds(0, d)], wk_v)
    load_v = load(w_keyval.at[:, pl.ds(d, d)], wv_v)
    load_o = load(w_out, wo_v.at[core])
    load_u = load(w_up, wu_v.at[core])
    load_d = load(w_down, wd_v.at[core])

    def send_all(src_at, dst, phase):
        def body(k, _):
            peer = lax.rem(chip + k, chips)
            pltpu.make_async_remote_copy(
                src_ref=src_at(peer),
                dst_ref=dst.at[chip],
                send_sem=send_sem.at[phase],
                recv_sem=recv_sem.at[phase],
                device_id={"dp": peer * 2 + core},
                device_id_type=MESH,
            ).start()
            return 0

        lax.fori_loop(1, chips, body, 0)

    def wait_all(ref, sem):
        part = ref.at[pl.ds(0, chips - 1)]
        pltpu.make_async_copy(part, part, sem).wait()

    for copy in load_gains:
        copy.wait()
    g_attn, g_mlp, g_post, b_post = [gains_v[i].reshape(1, d) for i in range(4)]

    load_first.wait()
    first = jnp.concatenate([first_v[s, 0:1, :].astype(F32) for s in range(SLOTS)], axis=0)
    rows_r[chip] = pack_rows(layer_norm(first, g_attn)).astype(BF16)
    pl.semaphore_wait(barrier, chips)
    send_all(lambda peer: rows_r.at[chip], rows_r, 0)

    shared = []
    for k, (src, dst) in enumerate(((w_query, wq_v), (w_out, wo_v), (w_up, wu_v), (w_down, wd_v))):
        copy = pltpu.make_async_remote_copy(
            src_ref=src,
            dst_ref=dst.at[core],
            send_sem=weight_send.at[k],
            recv_sem=weight_recv.at[k],
            device_id={"dp": sibling},
            device_id_type=MESH,
        )
        copy.start()
        shared.append(copy)
    share_q, share_o, share_u, share_d = shared

    whole = tok // 256 * 256

    def norm_tile(s):
        load_tiles[s].wait()

        def body(i, _):
            at = pl.ds(pl.multiple_of(i * 32, 32), 32)
            normed_v[s, at, :] = layer_norm(tiles_v[s, at, :].astype(F32), g_attn).astype(BF16)
            return 0

        lax.fori_loop(0, whole // 32, body, 0, unroll=2)
        tail = layer_norm(tiles_v[s, whole:tok, :].astype(F32), g_attn)
        tail = jnp.concatenate(
            [tail, jnp.zeros((normed_v.shape[1] - tok, d), F32)], axis=0
        )
        normed_v[s, whole:, :] = tail.astype(BF16)

    for s in range(SLOTS):
        norm_tile(s)

    load_q.wait()
    share_q.wait_recv()
    wait_all(rows_r, recv_sem.at[0])
    for g in range(groups):
        owners = size // ROWS
        packed = rows_r[g * owners : (g + 1) * owners].reshape(size, WIDE)
        each = spread(packed, d)
        for h in range(2):
            q = dot_t(each, wq_v[h]).astype(BF16)
            q_s[g * owners : (g + 1) * owners, h] = q.reshape(owners, ROWS, cw)
    send_all(lambda peer: q_s.at[peer], q_r, 1)
    q_r[chip] = q_s[chip]

    load_k.wait()
    wait_all(q_r, recv_sem.at[1])
    query = jnp.concatenate([q_r[i, h].astype(F32) for i in range(chips) for h in range(2)], axis=1)
    head_row = lax.broadcasted_iota(jnp.int32, (HEADS, d), 0)
    lane = lax.broadcasted_iota(jnp.int32, (HEADS, d), 1)
    own_head = (lane >= head_row * HEAD_DIM) & (lane < (head_row + 1) * HEAD_DIM)
    apart = jnp.concatenate(
        [jnp.where(own_head, query[s : s + 1], 0.0).astype(BF16) for s in range(SLOTS)], axis=0
    )
    keyed = dot_t(apart, wk_v[...]).astype(BF16)
    parts = [keyed[s * HEADS : (s + 1) * HEADS] for s in range(SLOTS)]
    scores = jnp.concatenate([dot_t(parts[s], normed_v[s, :whole, :]) for s in range(SLOTS)], axis=0)
    wide_keyed = keyed.astype(F32)
    extra = []
    for t in range(whole, tok):
        rows = [
            jnp.broadcast_to(normed_v[s, t : t + 1, :].astype(F32), (HEADS, d)) for s in range(SLOTS)
        ]
        extra.append(
            (rows, jnp.sum(wide_keyed * jnp.concatenate(rows, axis=0), axis=-1, keepdims=True))
        )
    scale = 1.0 / math.sqrt(HEAD_DIM)
    scores = scores * scale
    peak = jnp.max(scores, axis=-1, keepdims=True)
    for _, score in extra:
        peak = jnp.maximum(peak, score * scale)
    weights = jnp.exp(scores - peak)
    last = [jnp.exp(score * scale - peak) for _, score in extra]
    norm = 1.0 / (jnp.sum(weights, axis=-1, keepdims=True) + sum(last))
    weights = (weights * norm).astype(BF16)
    last = [(w * norm).astype(BF16).astype(F32) for w in last]
    context = []
    for s in range(SLOTS):
        at = slice(s * HEADS, (s + 1) * HEADS)
        mean = dot(weights[at], normed_v[s, :whole, :])
        for (rows, _), w in zip(extra, last):
            mean = mean + w[at] * rows[s]
        context.append(mean.astype(BF16))
    load_v.wait()
    valued = dot(jnp.concatenate(context, axis=0), wv_v[...])
    mixed = jnp.concatenate(
        [
            jnp.sum(
                jnp.where(own_head, valued[s * HEADS : (s + 1) * HEADS], 0.0),
                axis=0,
                keepdims=True,
            )
            for s in range(SLOTS)
        ],
        axis=0,
    )
    thrice = jnp.concatenate([mixed, mixed, mixed, mixed[0:1]], axis=0)
    for i in range(n):
        mix_s[i // 2, i % 2] = thrice[:, i * cw : (i + 1) * cw].astype(BF16)
    send_all(lambda peer: mix_s.at[peer], mix_r, 2)
    mix_r[chip] = mix_s[chip]

    load_o.wait()
    share_o.wait_recv()
    wait_all(mix_r, recv_sem.at[2])
    owners = size // ROWS
    for g in range(groups):
        at = slice(g * owners, (g + 1) * owners)
        part = dot(mix_r[at, 0].reshape(size, cw), wo_v[0])
        part = part + dot(mix_r[at, 1].reshape(size, cw), wo_v[1])
        out_s[at] = fold(part).astype(BF16).reshape(owners, ROWS, WIDE)
    send_all(lambda peer: out_s.at[peer], out_r, 3)
    out_r[chip] = out_s[chip]
    wait_all(out_r, recv_sem.at[3])

    def total_of(ref):
        acc = ref[0].astype(F32)
        for i in range(1, chips):
            acc = acc + ref[i].astype(F32)
        return unpack_rows(acc, d)

    settled = first + total_of(out_r)
    inner = layer_norm(settled, g_mlp)
    inner_r[chip] = pack_rows(inner).astype(BF16)
    send_all(lambda peer: inner_r.at[chip], inner_r, 4)
    load_u.wait()
    share_u.wait_recv()
    load_d.wait()
    share_d.wait_recv()
    wait_all(inner_r, recv_sem.at[4])
    for g in range(groups):
        at = slice(g * owners, (g + 1) * owners)
        rows = spread(inner_r[at].reshape(size, WIDE), d)
        hidden = gelu(dot_t(rows, wu_v[...].reshape(-1, d))).astype(BF16)
        feed_s[at] = fold(dot(hidden, wd_v[...].reshape(-1, d))).astype(BF16).reshape(owners, ROWS, WIDE)
    send_all(lambda peer: feed_s.at[peer], feed_r, 5)
    feed_r[chip] = feed_s[chip]
    wait_all(feed_r, recv_sem.at[5])

    outcome = settled + total_of(feed_r)
    final = layer_norm(outcome, g_post) + b_post
    count = counts[0]
    present = lax.broadcasted_iota(jnp.int32, (SLOTS, d), 0) < count
    summed = jnp.sum(jnp.where(present, final, 0.0), axis=0, keepdims=True)
    out[...] = summed / jnp.full((1, d), count, jnp.int32).astype(F32)

    for phase, ref in enumerate((rows_r, q_s, mix_s, out_s, inner_r, feed_s)):
        wait_all(ref, send_sem.at[phase])
    for copy in shared:
        copy.wait_send()


def shards(
    tiles, counts, w_query, w_keyval, w_out, w_up, w_down, gain_attn, gain_mlp, gain_post, bias_post
):
    n = lax.axis_size("dp")
    slots, tok, d = tiles.shape
    cw = w_query.shape[1]
    w_query, w_up = w_query.T, w_up.T
    padded = (tok + 15) // 16 * 16
    anywhere = pl.BlockSpec(memory_space=pl.ANY)
    vmem = pl.BlockSpec(memory_space=pltpu.VMEM)
    smem = pl.BlockSpec(memory_space=pltpu.SMEM)
    message = pltpu.VMEM((n // 2, ROWS, WIDE), BF16)
    narrow = pltpu.VMEM((n // 2, 2, ROWS, cw), BF16)
    return pl.pallas_call(
        functools.partial(kernel, n),
        out_shape=jax.ShapeDtypeStruct((counts.shape[0], d), F32),
        in_specs=[anywhere, smem] + [anywhere] * 9,
        out_specs=vmem,
        scratch_shapes=[
            pltpu.VMEM((4, d), F32),
            pltpu.VMEM((slots, 16, d), BF16),
            pltpu.VMEM((slots, tok, d), BF16),
            pltpu.VMEM((slots, padded, d), BF16),
            pltpu.VMEM((2,) + w_query.shape, BF16),
            pltpu.VMEM((d, d), BF16),
            pltpu.VMEM((d, d), BF16),
            pltpu.VMEM((2,) + w_out.shape, BF16),
            pltpu.VMEM((2,) + w_up.shape, BF16),
            pltpu.VMEM((2,) + w_down.shape, BF16),
            message, narrow, narrow, narrow, narrow, message, message, message, message, message,
            pltpu.SemaphoreType.DMA((16,)),
            pltpu.SemaphoreType.DMA((6,)),
            pltpu.SemaphoreType.DMA((6,)),
            pltpu.SemaphoreType.DMA((4,)),
            pltpu.SemaphoreType.DMA((4,)),
        ],
        compiler_params=pltpu.CompilerParams(
            collective_id=0, has_side_effects=True, vmem_limit_bytes=60 * 1024 * 1024
        ),
    )(tiles, counts, w_query, w_keyval, w_out, w_up, w_down, gain_attn, gain_mlp, gain_post, bias_post)


def solution(mesh):
    placed = (
        P(("groups", "dp"), None, None),
        P(("groups", "dp")),
        P(None, "dp"),
        P(),
        P("dp", None),
        P(None, "dp"),
        P("dp", None),
        P(),
        P(),
        P(),
        P(),
    )
    return jax.shard_map(
        shards, mesh=mesh, in_specs=placed, out_specs=P(("groups", "dp"), None), check_vma=False
    )
```

```python
import functools
import math

import jax
import jax.numpy as jnp
from jax import lax
from jax.experimental import pallas as pl
from jax.experimental.pallas import tpu as pltpu
from jax.sharding import PartitionSpec as P

HEADS = 16
HEAD_DIM = 80
SLOTS = 5
ROWS = 16
WIDE = 512
HALF = 256
PARTS = ((0, 3), (3, 5))
GROUP = 256

epsilon = 1e-05
F32 = jnp.float32
BF16 = jnp.bfloat16
MESH = pl.DeviceIdType.MESH


def layer_norm(values, gain):
    centre = jnp.mean(values, axis=-1, keepdims=True)
    centred = values - centre
    spread_sq = jnp.mean(centred * centred, axis=-1, keepdims=True)
    return centred * lax.rsqrt(spread_sq + epsilon) * gain


def erf(x):
    x = jnp.clip(x, -3.832506856900711, 3.832506856900711)
    sq = x * x
    top = jnp.full_like(x, 0.00022905065861350646)
    for c in (
        0.0034082910107109506,
        0.050955695062380861,
        0.18520832239976145,
        1.128379143519084,
    ):
        top = top * sq + c
    low = jnp.full_like(x, -1.1791602954361697e-7)
    for c in (
        0.000023547966471313185,
        0.0010179625278914885,
        0.014070470171167667,
        0.11098505178285362,
        0.49746925110067538,
        1.0,
    ):
        low = low * sq + c
    return x * top / low


def gelu(x):
    return 0.5 * x * (1.0 + erf(x * math.sqrt(0.5)))


def dot(a, b):
    return jnp.dot(a, b, preferred_element_type=F32)


def dot_t(a, b):
    return lax.dot_general(a, b, (((1,), (1,)), ((), ())), preferred_element_type=F32)


def pack_rows(x, wide):
    slots, d = x.shape
    blocks = -(-d // wide)
    pieces = [x[:, c * wide : (c + 1) * wide] for c in range(blocks)]
    if blocks * wide > d:
        short = jnp.zeros((slots, blocks * wide - d), F32)
        pieces[-1] = jnp.concatenate([pieces[-1], short], axis=1)
    pieces.append(jnp.zeros((ROWS - slots * blocks, wide), F32))
    return jnp.concatenate(pieces, axis=0)


def unpack_rows(p, slots, d):
    wide = p.shape[1]
    blocks = -(-d // wide)
    return jnp.concatenate(
        [p[c * slots : (c + 1) * slots, : min(wide, d - c * wide)] for c in range(blocks)], axis=1
    )


def pick(size, slots, offset):
    r = lax.broadcasted_iota(jnp.int32, (size, size), 0)
    c = lax.broadcasted_iota(jnp.int32, (size, size), 1)
    rm = r & 15
    slot = rm
    for k in range(slots, ROWS, slots):
        slot = slot - jnp.where(rm >= k, slots, 0)
    return jnp.where(((r >> 4) == (c >> 4)) & ((c & 15) == slot + offset), 1.0, 0.0).astype(BF16)


def spread(packed, slots, d):
    size, wide = packed.shape
    out = []
    for c in range(-(-d // wide)):
        src = packed[:, : min(wide, d - c * wide)]
        out.append(dot(pick(size, slots, c * slots), src).astype(BF16))
    return jnp.concatenate(out, axis=1)


def fold(y, slots, wide):
    size, d = y.shape
    blocks = d // wide
    rm = lax.broadcasted_iota(jnp.int32, (size, wide), 0) & 15
    out = y[:, (blocks - 1) * wide :]
    for c in range(blocks - 2, -1, -1):
        out = jnp.where(rm < (c + 1) * slots, y[:, c * wide : (c + 1) * wide], out)
    return out


def kernel(
    n,
    tiles, counts, w_query, w_keyval, w_out, w_up, w_down, gain_attn, gain_mlp, gain_post, bias_post,
    out,
    gains_v, first_v, tiles_v, normed_v, wq_v, wk_v, wv_v, wo_v, wu_v, wd_v,
    rows_r, q_s, q_r, mix_s, mix_r, out_s, out_r, inner_r, feed_s, feed_r,
    load_sem, send_sem, recv_sem, weight_send, weight_recv,
):
    me = lax.axis_index("dp")
    tok, d = tiles.shape[1], tiles.shape[2]
    cw = w_query.shape[0]
    core = lax.rem(me, 2)
    sibling = me + 1 - 2 * core
    chips = n // 2
    chip = lax.div(me, 2)
    total = chips * ROWS
    groups = max(total // GROUP, 1)
    size = total // groups

    barrier = pltpu.get_barrier_semaphore()

    def greet(k, _):
        peer = lax.rem(chip + k, chips) * 2 + core
        pl.semaphore_signal(barrier, inc=1, device_id={"dp": peer}, device_id_type=MESH)
        return 0

    pl.semaphore_signal(barrier, inc=1, device_id={"dp": sibling}, device_id_type=MESH)
    lax.fori_loop(1, chips, greet, 0)

    loads = []

    def load(src, dst):
        copy = pltpu.make_async_copy(src, dst, load_sem.at[len(loads)])
        copy.start()
        loads.append(copy)
        return copy

    load_gains = [
        load(ref, gains_v.at[i])
        for i, ref in enumerate((gain_attn, gain_mlp, gain_post, bias_post))
    ]
    load_first = load(tiles.at[:, pl.ds(0, 16), :], first_v)
    load_q = load(w_query, wq_v.at[core])
    load_tiles = [load(tiles.at[s], tiles_v.at[s]) for s in range(SLOTS)]
    load_k = load(w_keyval.at[:, pl.ds(0, d)], wk_v)
    load_v = load(w_keyval.at[:, pl.ds(d, d)], wv_v)
    load_o = load(w_out, wo_v.at[core])
    load_u = load(w_up, wu_v.at[core])
    load_d = load(w_down, wd_v.at[core])

    def send_all(src_at, dst, phase):
        def body(k, _):
            peer = lax.rem(chip + k, chips)
            pltpu.make_async_remote_copy(
                src_ref=src_at(peer),
                dst_ref=dst.at[chip],
                send_sem=send_sem.at[phase],
                recv_sem=recv_sem.at[phase],
                device_id={"dp": peer * 2 + core},
                device_id_type=MESH,
            ).start()
            return 0

        lax.fori_loop(1, chips, body, 0)

    def wait_all(ref, sem):
        part = ref.at[pl.ds(0, chips - 1)]
        pltpu.make_async_copy(part, part, sem).wait()

    for copy in load_gains:
        copy.wait()
    g_attn, g_mlp, g_post, b_post = [gains_v[i].reshape(1, d) for i in range(4)]

    load_first.wait()
    first = jnp.concatenate([first_v[s, 0:1, :].astype(F32) for s in range(SLOTS)], axis=0)
    rows_r[chip] = pack_rows(layer_norm(first, g_attn), WIDE).astype(BF16)
    pl.semaphore_wait(barrier, chips)
    send_all(lambda peer: rows_r.at[chip], rows_r, 0)

    shared = []
    for k, (src, dst) in enumerate(((w_query, wq_v), (w_out, wo_v), (w_up, wu_v), (w_down, wd_v))):
        copy = pltpu.make_async_remote_copy(
            src_ref=src,
            dst_ref=dst.at[core],
            send_sem=weight_send.at[k],
            recv_sem=weight_recv.at[k],
            device_id={"dp": sibling},
            device_id_type=MESH,
        )
        copy.start()
        shared.append(copy)
    share_q, share_o, share_u, share_d = shared

    whole = tok // 256 * 256

    def norm_tile(s):
        load_tiles[s].wait()

        def body(i, _):
            at = pl.ds(pl.multiple_of(i * 32, 32), 32)
            normed_v[s, at, :] = layer_norm(tiles_v[s, at, :].astype(F32), g_attn).astype(BF16)
            return 0

        lax.fori_loop(0, whole // 32, body, 0, unroll=2)
        tail = layer_norm(tiles_v[s, whole:tok, :].astype(F32), g_attn)
        tail = jnp.concatenate(
            [tail, jnp.zeros((normed_v.shape[1] - tok, d), F32)], axis=0
        )
        normed_v[s, whole:, :] = tail.astype(BF16)

    for s in range(SLOTS):
        norm_tile(s)

    load_q.wait()
    share_q.wait_recv()
    wait_all(rows_r, recv_sem.at[0])
    for g in range(groups):
        owners = size // ROWS
        packed = rows_r[g * owners : (g + 1) * owners].reshape(size, WIDE)
        each = spread(packed, SLOTS, d)
        for h in range(2):
            q = dot_t(each, wq_v[h]).astype(BF16)
            q_s[g * owners : (g + 1) * owners, h] = q.reshape(owners, ROWS, cw)
    send_all(lambda peer: q_s.at[peer], q_r, 1)
    q_r[chip] = q_s[chip]

    load_k.wait()
    wait_all(q_r, recv_sem.at[1])
    query = jnp.concatenate([q_r[i, h].astype(F32) for i in range(chips) for h in range(2)], axis=1)
    head_row = lax.broadcasted_iota(jnp.int32, (HEADS, d), 0)
    lane = lax.broadcasted_iota(jnp.int32, (HEADS, d), 1)
    own_head = (lane >= head_row * HEAD_DIM) & (lane < (head_row + 1) * HEAD_DIM)
    apart = jnp.concatenate(
        [jnp.where(own_head, query[s : s + 1], 0.0).astype(BF16) for s in range(SLOTS)], axis=0
    )
    keyed = dot_t(apart, wk_v[...]).astype(BF16)
    parts = [keyed[s * HEADS : (s + 1) * HEADS] for s in range(SLOTS)]
    scores = jnp.concatenate([dot_t(parts[s], normed_v[s, :whole, :]) for s in range(SLOTS)], axis=0)
    wide_keyed = keyed.astype(F32)
    extra = []
    for t in range(whole, tok):
        rows = [
            jnp.broadcast_to(normed_v[s, t : t + 1, :].astype(F32), (HEADS, d)) for s in range(SLOTS)
        ]
        extra.append(
            (rows, jnp.sum(wide_keyed * jnp.concatenate(rows, axis=0), axis=-1, keepdims=True))
        )
    scale = 1.0 / math.sqrt(HEAD_DIM)
    scores = scores * scale
    peak = jnp.max(scores, axis=-1, keepdims=True)
    for _, score in extra:
        peak = jnp.maximum(peak, score * scale)
    weights = jnp.exp(scores - peak)
    last = [jnp.exp(score * scale - peak) for _, score in extra]
    norm = 1.0 / (jnp.sum(weights, axis=-1, keepdims=True) + sum(last))
    weights = (weights * norm).astype(BF16)
    last = [(w * norm).astype(BF16).astype(F32) for w in last]
    context = []
    for s in range(SLOTS):
        at = slice(s * HEADS, (s + 1) * HEADS)
        mean = dot(weights[at], normed_v[s, :whole, :])
        for (rows, _), w in zip(extra, last):
            mean = mean + w[at] * rows[s]
        context.append(mean.astype(BF16))
    load_v.wait()
    valued = dot(jnp.concatenate(context, axis=0), wv_v[...])
    mixed = jnp.concatenate(
        [
            jnp.sum(
                jnp.where(own_head, valued[s * HEADS : (s + 1) * HEADS], 0.0),
                axis=0,
                keepdims=True,
            )
            for s in range(SLOTS)
        ],
        axis=0,
    )
    thrice = jnp.concatenate([mixed, mixed, mixed, mixed[0:1]], axis=0)
    for i in range(n):
        mix_s[i // 2, i % 2] = thrice[:, i * cw : (i + 1) * cw].astype(BF16)
    send_all(lambda peer: mix_s.at[peer], mix_r, 2)
    mix_r[chip] = mix_s[chip]

    load_o.wait()
    share_o.wait_recv()
    wait_all(mix_r, recv_sem.at[2])
    owners = size // ROWS
    spans = [slice(g * owners, (g + 1) * owners) for g in range(groups)]
    for h, (low, high) in enumerate(PARTS):
        slots = high - low
        for at in spans:
            moved = pick(size, slots, low)
            part = 0.0
            for c in range(2):
                column = dot(moved, mix_r[at, c].reshape(size, cw)).astype(BF16)
                part = part + dot(column, wo_v[c])
            out_s[h, at] = fold(part, slots, HALF).astype(BF16).reshape(owners, ROWS, HALF)
        send_all(lambda peer: out_s.at[h, peer], out_r.at[h], 3 + h)
        out_r[h, chip] = out_s[h, chip]

    def total_of(ref, h, slots):
        acc = ref[h, 0].astype(F32)
        for i in range(1, chips):
            acc = acc + ref[h, i].astype(F32)
        return unpack_rows(acc, slots, d)

    settled = []
    for h, (low, high) in enumerate(PARTS):
        wait_all(out_r.at[h], recv_sem.at[3 + h])
        settled.append(first[low:high] + total_of(out_r, h, high - low))
        inner_r[h, chip] = pack_rows(layer_norm(settled[h], g_mlp), HALF).astype(BF16)
        send_all(lambda peer: inner_r.at[h, chip], inner_r.at[h], 5 + h)

    load_u.wait()
    share_u.wait_recv()
    load_d.wait()
    share_d.wait_recv()
    for h, (low, high) in enumerate(PARTS):
        slots = high - low
        wait_all(inner_r.at[h], recv_sem.at[5 + h])
        for at in spans:
            rows = spread(inner_r[h, at].reshape(size, HALF), slots, d)
            hidden = gelu(dot_t(rows, wu_v[...].reshape(-1, d))).astype(BF16)
            feed = dot(hidden, wd_v[...].reshape(-1, d))
            feed_s[h, at] = fold(feed, slots, HALF).astype(BF16).reshape(owners, ROWS, HALF)
        send_all(lambda peer: feed_s.at[h, peer], feed_r.at[h], 7 + h)
        feed_r[h, chip] = feed_s[h, chip]

    count = counts[0]
    summed = jnp.zeros((1, d), F32)
    for h, (low, high) in enumerate(PARTS):
        wait_all(feed_r.at[h], recv_sem.at[7 + h])
        outcome = settled[h] + total_of(feed_r, h, high - low)
        final = layer_norm(outcome, g_post) + b_post
        present = lax.broadcasted_iota(jnp.int32, (high - low, d), 0) + low < count
        summed = summed + jnp.sum(jnp.where(present, final, 0.0), axis=0, keepdims=True)
    out[...] = summed / jnp.full((1, d), count, jnp.int32).astype(F32)

    sent = [rows_r, q_s, mix_s]
    for ref in (out_s, inner_r, feed_s):
        sent += [ref.at[0], ref.at[1]]
    for phase, ref in enumerate(sent):
        wait_all(ref, send_sem.at[phase])
    for copy in shared:
        copy.wait_send()


def shards(
    tiles, counts, w_query, w_keyval, w_out, w_up, w_down, gain_attn, gain_mlp, gain_post, bias_post
):
    n = lax.axis_size("dp")
    slots, tok, d = tiles.shape
    cw = w_query.shape[1]
    w_query, w_up = w_query.T, w_up.T
    padded = (tok + 15) // 16 * 16
    anywhere = pl.BlockSpec(memory_space=pl.ANY)
    vmem = pl.BlockSpec(memory_space=pltpu.VMEM)
    smem = pl.BlockSpec(memory_space=pltpu.SMEM)
    message = pltpu.VMEM((n // 2, ROWS, WIDE), BF16)
    halved = pltpu.VMEM((2, n // 2, ROWS, HALF), BF16)
    narrow = pltpu.VMEM((n // 2, 2, ROWS, cw), BF16)
    return pl.pallas_call(
        functools.partial(kernel, n),
        out_shape=jax.ShapeDtypeStruct((counts.shape[0], d), F32),
        in_specs=[anywhere, smem] + [anywhere] * 9,
        out_specs=vmem,
        scratch_shapes=[
            pltpu.VMEM((4, d), F32),
            pltpu.VMEM((slots, 16, d), BF16),
            pltpu.VMEM((slots, tok, d), BF16),
            pltpu.VMEM((slots, padded, d), BF16),
            pltpu.VMEM((2,) + w_query.shape, BF16),
            pltpu.VMEM((d, d), BF16),
            pltpu.VMEM((d, d), BF16),
            pltpu.VMEM((2,) + w_out.shape, BF16),
            pltpu.VMEM((2,) + w_up.shape, BF16),
            pltpu.VMEM((2,) + w_down.shape, BF16),
            message, narrow, narrow, narrow, narrow, halved, halved, halved, halved, halved,
            pltpu.SemaphoreType.DMA((16,)),
            pltpu.SemaphoreType.DMA((9,)),
            pltpu.SemaphoreType.DMA((9,)),
            pltpu.SemaphoreType.DMA((4,)),
            pltpu.SemaphoreType.DMA((4,)),
        ],
        compiler_params=pltpu.CompilerParams(
            collective_id=0, has_side_effects=True, vmem_limit_bytes=60 * 1024 * 1024
        ),
    )(tiles, counts, w_query, w_keyval, w_out, w_up, w_down, gain_attn, gain_mlp, gain_post, bias_post)


def solution(mesh):
    placed = (
        P(("groups", "dp"), None, None),
        P(("groups", "dp")),
        P(None, "dp"),
        P(),
        P("dp", None),
        P(None, "dp"),
        P("dp", None),
        P(),
        P(),
        P(),
        P(),
    )
    return jax.shard_map(
        shards, mesh=mesh, in_specs=placed, out_specs=P(("groups", "dp"), None), check_vma=False
    )
```

```python
import functools
import math

import jax
import jax.numpy as jnp
from jax import lax
from jax.experimental import pallas as pl
from jax.experimental.pallas import tpu as pltpu
from jax.sharding import PartitionSpec as P

HEADS = 16
HEAD_DIM = 80
SLOTS = 5
ROWS = 16
WIDE = 512
HALF = 256
PARTS = ((0, 3), (3, 5))
GROUP = 256

epsilon = 1e-05
F32 = jnp.float32
BF16 = jnp.bfloat16
MESH = pl.DeviceIdType.MESH


def layer_norm(values, gain):
    centre = jnp.mean(values, axis=-1, keepdims=True)
    centred = values - centre
    spread_sq = jnp.mean(centred * centred, axis=-1, keepdims=True)
    return centred * lax.rsqrt(spread_sq + epsilon) * gain


def erf(x):
    x = jnp.clip(x, -3.832506856900711, 3.832506856900711)
    sq = x * x
    top = jnp.full_like(x, 0.00022905065861350646)
    for c in (
        0.0034082910107109506,
        0.050955695062380861,
        0.18520832239976145,
        1.128379143519084,
    ):
        top = top * sq + c
    low = jnp.full_like(x, -1.1791602954361697e-7)
    for c in (
        0.000023547966471313185,
        0.0010179625278914885,
        0.014070470171167667,
        0.11098505178285362,
        0.49746925110067538,
        1.0,
    ):
        low = low * sq + c
    return x * top / low


def gelu(x):
    return 0.5 * x * (1.0 + erf(x * math.sqrt(0.5)))


def dot(a, b):
    return jnp.dot(a, b, preferred_element_type=F32)


def dot_t(a, b):
    return lax.dot_general(a, b, (((1,), (1,)), ((), ())), preferred_element_type=F32)


def pack_rows(x, wide):
    slots, d = x.shape
    blocks = -(-d // wide)
    pieces = [x[:, c * wide : (c + 1) * wide] for c in range(blocks)]
    if blocks * wide > d:
        short = jnp.zeros((slots, blocks * wide - d), F32)
        pieces[-1] = jnp.concatenate([pieces[-1], short], axis=1)
    pieces.append(jnp.zeros((ROWS - slots * blocks, wide), F32))
    return jnp.concatenate(pieces, axis=0)


def unpack_rows(p, slots, d):
    wide = p.shape[1]
    blocks = -(-d // wide)
    return jnp.concatenate(
        [p[c * slots : (c + 1) * slots, : min(wide, d - c * wide)] for c in range(blocks)], axis=1
    )


def pick(size, slots, offset):
    r = lax.broadcasted_iota(jnp.int32, (size, size), 0)
    c = lax.broadcasted_iota(jnp.int32, (size, size), 1)
    rm = r & 15
    slot = rm
    for k in range(slots, ROWS, slots):
        slot = slot - jnp.where(rm >= k, slots, 0)
    return jnp.where(((r >> 4) == (c >> 4)) & ((c & 15) == slot + offset), 1.0, 0.0).astype(BF16)


def spread(packed, slots, d):
    size, wide = packed.shape
    out = []
    for c in range(-(-d // wide)):
        src = packed[:, : min(wide, d - c * wide)]
        out.append(dot(pick(size, slots, c * slots), src).astype(BF16))
    return jnp.concatenate(out, axis=1)


def fold(y, slots, wide):
    size, d = y.shape
    blocks = d // wide
    rm = lax.broadcasted_iota(jnp.int32, (size, wide), 0) & 15
    out = y[:, (blocks - 1) * wide :]
    for c in range(blocks - 2, -1, -1):
        out = jnp.where(rm < (c + 1) * slots, y[:, c * wide : (c + 1) * wide], out)
    return out


def kernel(
    n,
    tiles, counts, w_query, w_keyval, w_out, w_up, w_down, gain_attn, gain_mlp, gain_post, bias_post,
    out,
    gains_v, first_v, tiles_v, normed_v, wq_v, wk_v, wv_v, wo_v, wu_v, wd_v,
    rows_r, q_s, q_r, mix_s, mix_r, out_s, out_r, inner_r, feed_s, feed_r,
    load_sem, send_sem, recv_sem, weight_send, weight_recv,
):
    me = lax.axis_index("dp")
    tok, d = tiles.shape[1], tiles.shape[2]
    cw = w_query.shape[0]
    core = lax.rem(me, 2)
    sibling = me + 1 - 2 * core
    chips = n // 2
    chip = lax.div(me, 2)
    total = chips * ROWS
    groups = max(total // GROUP, 1)
    size = total // groups

    barrier = pltpu.get_barrier_semaphore()

    def greet(k, _):
        peer = lax.rem(chip + k, chips) * 2 + core
        pl.semaphore_signal(barrier, inc=1, device_id={"dp": peer}, device_id_type=MESH)
        return 0

    pl.semaphore_signal(barrier, inc=1, device_id={"dp": sibling}, device_id_type=MESH)
    lax.fori_loop(1, chips, greet, 0)

    loads = []

    def load(src, dst):
        copy = pltpu.make_async_copy(src, dst, load_sem.at[len(loads)])
        copy.start()
        loads.append(copy)
        return copy

    load_gains = [
        load(ref, gains_v.at[i])
        for i, ref in enumerate((gain_attn, gain_mlp, gain_post, bias_post))
    ]
    load_first = load(tiles.at[:, pl.ds(0, 16), :], first_v)
    load_q = load(w_query, wq_v.at[core])
    load_tiles = [load(tiles.at[s], tiles_v.at[s]) for s in range(SLOTS)]
    load_k = load(w_keyval.at[:, pl.ds(0, d)], wk_v)
    load_v = load(w_keyval.at[:, pl.ds(d, d)], wv_v)
    load_o = load(w_out, wo_v.at[core])
    load_u = load(w_up, wu_v.at[core])
    load_d = load(w_down, wd_v.at[core])

    def send_all(src_at, dst, phase):
        def body(k, _):
            peer = lax.rem(chip + k, chips)
            pltpu.make_async_remote_copy(
                src_ref=src_at(peer),
                dst_ref=dst.at[chip],
                send_sem=send_sem.at[phase],
                recv_sem=recv_sem.at[phase],
                device_id={"dp": peer * 2 + core},
                device_id_type=MESH,
            ).start()
            return 0

        lax.fori_loop(1, chips, body, 0)

    def wait_all(ref, sem):
        part = ref.at[pl.ds(0, chips - 1)]
        pltpu.make_async_copy(part, part, sem).wait()

    for copy in load_gains:
        copy.wait()
    g_attn, g_mlp, g_post, b_post = [gains_v[i].reshape(1, d) for i in range(4)]

    load_first.wait()
    first = jnp.concatenate([first_v[s, 0:1, :].astype(F32) for s in range(SLOTS)], axis=0)
    rows_r[chip] = pack_rows(layer_norm(first, g_attn), WIDE).astype(BF16)
    pl.semaphore_wait(barrier, chips)
    send_all(lambda peer: rows_r.at[chip], rows_r, 0)

    shared = []
    for k, (src, dst) in enumerate(((w_query, wq_v), (w_out, wo_v), (w_up, wu_v), (w_down, wd_v))):
        copy = pltpu.make_async_remote_copy(
            src_ref=src,
            dst_ref=dst.at[core],
            send_sem=weight_send.at[k],
            recv_sem=weight_recv.at[k],
            device_id={"dp": sibling},
            device_id_type=MESH,
        )
        copy.start()
        shared.append(copy)
    share_q, share_o, share_u, share_d = shared

    whole = tok // 256 * 256

    def norm_tile(s):
        load_tiles[s].wait()

        def body(i, _):
            at = pl.ds(pl.multiple_of(i * 32, 32), 32)
            normed_v[s, at, :] = layer_norm(tiles_v[s, at, :].astype(F32), g_attn).astype(BF16)
            return 0

        lax.fori_loop(0, whole // 32, body, 0, unroll=2)
        tail = layer_norm(tiles_v[s, whole:tok, :].astype(F32), g_attn)
        tail = jnp.concatenate(
            [tail, jnp.zeros((normed_v.shape[1] - tok, d), F32)], axis=0
        )
        normed_v[s, whole:, :] = tail.astype(BF16)

    for s in range(SLOTS):
        norm_tile(s)

    load_q.wait()
    share_q.wait_recv()
    wait_all(rows_r, recv_sem.at[0])
    for g in range(groups):
        owners = size // ROWS
        packed = rows_r[g * owners : (g + 1) * owners].reshape(size, WIDE)
        each = spread(packed, SLOTS, d)
        upper = (lax.broadcasted_iota(jnp.int32, (size, cw), 0) & 15) < SLOTS
        q = jnp.where(upper, dot_t(each, wq_v[0]), dot_t(each, wq_v[1])).astype(BF16)
        q_s[g * owners : (g + 1) * owners] = q.reshape(owners, ROWS, cw)
    send_all(lambda peer: q_s.at[peer], q_r, 1)
    q_r[chip] = q_s[chip]

    load_k.wait()
    wait_all(q_r, recv_sem.at[1])
    query = jnp.concatenate([
            q_r[i].astype(F32)[h * SLOTS : (h + 1) * SLOTS] for i in range(chips) for h in range(2)
        ], axis=1)
    head_row = lax.broadcasted_iota(jnp.int32, (HEADS, d), 0)
    lane = lax.broadcasted_iota(jnp.int32, (HEADS, d), 1)
    own_head = (lane >= head_row * HEAD_DIM) & (lane < (head_row + 1) * HEAD_DIM)
    apart = jnp.concatenate(
        [jnp.where(own_head, query[s : s + 1], 0.0).astype(BF16) for s in range(SLOTS)], axis=0
    )
    keyed = dot_t(apart, wk_v[...]).astype(BF16)
    parts = [keyed[s * HEADS : (s + 1) * HEADS] for s in range(SLOTS)]
    scores = jnp.concatenate([dot_t(parts[s], normed_v[s, :whole, :]) for s in range(SLOTS)], axis=0)
    wide_keyed = keyed.astype(F32)
    extra = []
    for t in range(whole, tok):
        rows = [
            jnp.broadcast_to(normed_v[s, t : t + 1, :].astype(F32), (HEADS, d)) for s in range(SLOTS)
        ]
        extra.append(
            (rows, jnp.sum(wide_keyed * jnp.concatenate(rows, axis=0), axis=-1, keepdims=True))
        )
    scale = 1.0 / math.sqrt(HEAD_DIM)
    scores = scores * scale
    peak = jnp.max(scores, axis=-1, keepdims=True)
    for _, score in extra:
        peak = jnp.maximum(peak, score * scale)
    weights = jnp.exp(scores - peak)
    last = [jnp.exp(score * scale - peak) for _, score in extra]
    norm = 1.0 / (jnp.sum(weights, axis=-1, keepdims=True) + sum(last))
    weights = (weights * norm).astype(BF16)
    last = [(w * norm).astype(BF16).astype(F32) for w in last]
    context = []
    for s in range(SLOTS):
        at = slice(s * HEADS, (s + 1) * HEADS)
        mean = dot(weights[at], normed_v[s, :whole, :])
        for (rows, _), w in zip(extra, last):
            mean = mean + w[at] * rows[s]
        context.append(mean.astype(BF16))
    load_v.wait()
    valued = dot(jnp.concatenate(context, axis=0), wv_v[...])
    mixed = jnp.concatenate(
        [
            jnp.sum(
                jnp.where(own_head, valued[s * HEADS : (s + 1) * HEADS], 0.0),
                axis=0,
                keepdims=True,
            )
            for s in range(SLOTS)
        ],
        axis=0,
    )
    spare = jnp.zeros((ROWS - 2 * SLOTS, cw), F32)
    for i in range(chips):
        pair = [mixed[:, c * cw : (c + 1) * cw] for c in (2 * i, 2 * i + 1)]
        mix_s[i] = jnp.concatenate(pair + [spare], axis=0).astype(BF16)
    send_all(lambda peer: mix_s.at[peer], mix_r, 2)
    mix_r[chip] = mix_s[chip]

    load_o.wait()
    share_o.wait_recv()
    wait_all(mix_r, recv_sem.at[2])
    owners = size // ROWS
    spans = [slice(g * owners, (g + 1) * owners) for g in range(groups)]
    for h, (low, high) in enumerate(PARTS):
        slots = high - low
        for at in spans:
            part = 0.0
            for c in range(2):
                moved = pick(size, slots, low + c * SLOTS)
                column = dot(moved, mix_r[at].reshape(size, cw)).astype(BF16)
                part = part + dot(column, wo_v[c])
            out_s[h, at] = fold(part, slots, HALF).astype(BF16).reshape(owners, ROWS, HALF)
        send_all(lambda peer: out_s.at[h, peer], out_r.at[h], 3 + h)
        out_r[h, chip] = out_s[h, chip]

    def total_of(ref, h, slots):
        acc = ref[h, 0].astype(F32)
        for i in range(1, chips):
            acc = acc + ref[h, i].astype(F32)
        return unpack_rows(acc, slots, d)

    settled = []
    for h, (low, high) in enumerate(PARTS):
        wait_all(out_r.at[h], recv_sem.at[3 + h])
        settled.append(first[low:high] + total_of(out_r, h, high - low))
        inner_r[h, chip] = pack_rows(layer_norm(settled[h], g_mlp), HALF).astype(BF16)
        send_all(lambda peer: inner_r.at[h, chip], inner_r.at[h], 5 + h)

    load_u.wait()
    share_u.wait_recv()
    load_d.wait()
    share_d.wait_recv()
    for h, (low, high) in enumerate(PARTS):
        slots = high - low
        wait_all(inner_r.at[h], recv_sem.at[5 + h])
        for at in spans:
            rows = spread(inner_r[h, at].reshape(size, HALF), slots, d)
            hidden = gelu(dot_t(rows, wu_v[...].reshape(-1, d))).astype(BF16)
            feed = dot(hidden, wd_v[...].reshape(-1, d))
            feed_s[h, at] = fold(feed, slots, HALF).astype(BF16).reshape(owners, ROWS, HALF)
        send_all(lambda peer: feed_s.at[h, peer], feed_r.at[h], 7 + h)
        feed_r[h, chip] = feed_s[h, chip]

    count = counts[0]
    summed = jnp.zeros((1, d), F32)
    for h, (low, high) in enumerate(PARTS):
        wait_all(feed_r.at[h], recv_sem.at[7 + h])
        outcome = settled[h] + total_of(feed_r, h, high - low)
        final = layer_norm(outcome, g_post) + b_post
        present = lax.broadcasted_iota(jnp.int32, (high - low, d), 0) + low < count
        summed = summed + jnp.sum(jnp.where(present, final, 0.0), axis=0, keepdims=True)
    out[...] = summed / jnp.full((1, d), count, jnp.int32).astype(F32)

    sent = [rows_r, q_s, mix_s]
    for ref in (out_s, inner_r, feed_s):
        sent += [ref.at[0], ref.at[1]]
    for phase, ref in enumerate(sent):
        wait_all(ref, send_sem.at[phase])
    for copy in shared:
        copy.wait_send()


def shards(
    tiles, counts, w_query, w_keyval, w_out, w_up, w_down, gain_attn, gain_mlp, gain_post, bias_post
):
    n = lax.axis_size("dp")
    slots, tok, d = tiles.shape
    cw = w_query.shape[1]
    w_query, w_up = w_query.T, w_up.T
    padded = (tok + 15) // 16 * 16
    anywhere = pl.BlockSpec(memory_space=pl.ANY)
    vmem = pl.BlockSpec(memory_space=pltpu.VMEM)
    smem = pl.BlockSpec(memory_space=pltpu.SMEM)
    message = pltpu.VMEM((n // 2, ROWS, WIDE), BF16)
    halved = pltpu.VMEM((2, n // 2, ROWS, HALF), BF16)
    narrow = pltpu.VMEM((n // 2, ROWS, cw), BF16)
    return pl.pallas_call(
        functools.partial(kernel, n),
        out_shape=jax.ShapeDtypeStruct((counts.shape[0], d), F32),
        in_specs=[anywhere, smem] + [anywhere] * 9,
        out_specs=vmem,
        scratch_shapes=[
            pltpu.VMEM((4, d), F32),
            pltpu.VMEM((slots, 16, d), BF16),
            pltpu.VMEM((slots, tok, d), BF16),
            pltpu.VMEM((slots, padded, d), BF16),
            pltpu.VMEM((2,) + w_query.shape, BF16),
            pltpu.VMEM((d, d), BF16),
            pltpu.VMEM((d, d), BF16),
            pltpu.VMEM((2,) + w_out.shape, BF16),
            pltpu.VMEM((2,) + w_up.shape, BF16),
            pltpu.VMEM((2,) + w_down.shape, BF16),
            message, narrow, narrow, narrow, narrow, halved, halved, halved, halved, halved,
            pltpu.SemaphoreType.DMA((16,)),
            pltpu.SemaphoreType.DMA((9,)),
            pltpu.SemaphoreType.DMA((9,)),
            pltpu.SemaphoreType.DMA((4,)),
            pltpu.SemaphoreType.DMA((4,)),
        ],
        compiler_params=pltpu.CompilerParams(
            collective_id=0, has_side_effects=True, vmem_limit_bytes=60 * 1024 * 1024
        ),
    )(tiles, counts, w_query, w_keyval, w_out, w_up, w_down, gain_attn, gain_mlp, gain_post, bias_post)


def solution(mesh):
    placed = (
        P(("groups", "dp"), None, None),
        P(("groups", "dp")),
        P(None, "dp"),
        P(),
        P("dp", None),
        P(None, "dp"),
        P("dp", None),
        P(),
        P(),
        P(),
        P(),
    )
    return jax.shard_map(
        shards, mesh=mesh, in_specs=placed, out_specs=P(("groups", "dp"), None), check_vma=False
    )
```
